32 devices in a mesh: ctx: 8 (over y, x, core), head: 4 (over z).
Axes of the slice: x: 2, y: 2, z: 4, core: 2. Of those that a mesh axis runs over, the one named last changes fastest.
Arguments:
- queries: bfloat16 [1024, 4096], P('ctx', 'head'), may hold values from -6 to 6
- key_input: bfloat16 [2, 1024, 4096], P(None, 'ctx', 'head'), may hold values from -6 to 6
- value_input: bfloat16 [2, 1024, 4096], P(None, 'ctx', 'head'), may hold values from -6 to 6
- beta_rates: float32 [32, 2, 1024], P('head', None, 'ctx'), may hold values from 0 to 1.9, as said below
- out_grad: bfloat16 [1024, 4096], P(('ctx', 'head')), may hold values from -0.75 to 0.75
- out_weight: bfloat16 [4096, 4096], P('head'), may hold values from -0.09375 to 0.09375
Outputs:
- grad_queries: bfloat16 [1024, 4096], P('ctx', 'head')
- grad_keys: bfloat16 [2, 1024, 4096], P(None, 'ctx', 'head')
- grad_values: bfloat16 [2, 1024, 4096], P(None, 'ctx', 'head')
- grad_rates: float32 [32, 2, 1024], P('head', None, 'ctx')
The draws below stay inside these ranges and needn't reach their ends.
Inputs may be any that keep to these rules, and one draw needn't show every extreme that they name: `beta_rates`: positive strengths.
All inputs are finite; a program needn't handle non-finite values.
Results may differ from the reference program's by a relative error of at most 0.011.
Values may be sent and summed in bfloat16 or wider, within the bound.
A program may use at most 192 MiB of HBM per device.

```python
import jax
import jax.numpy as jnp
from jax import lax

D = 4096
HEADS = 32
HEAD_DIM = 128
HOUSE = 2
BLOCK = 64
TOKENS = 1024


def draw_beta_rates(key, part):
    pick_key, slow_key, fast_key, jitter_key = jax.random.split(key, 4)
    slow_share = 0.5
    slow_heads = jax.random.uniform(pick_key, (HEADS, 1, 1)) < slow_share
    base_rate = HEAD_DIM / (HOUSE * TOKENS)
    slow_rate = base_rate * jnp.exp(jax.random.uniform(slow_key, (HEADS, 1, 1), minval=jnp.log(0.05), maxval=0.0))
    fast_rate = jnp.exp(jax.random.uniform(fast_key, (HEADS, 1, 1), minval=jnp.log(0.3), maxval=jnp.log(1.5)))
    jitter = jnp.exp(jax.random.uniform(jitter_key, (HEADS, HOUSE, TOKENS), minval=-0.7, maxval=0.7))
    rates = jnp.where(slow_heads, slow_rate, fast_rate) * jitter
    return jnp.clip(rates, 1e-06, 1.9).astype(jnp.float32)


def levels(rng, shape, cuts, low, top_value):
    gain = 1.0
    for dim, blocks in cuts:
        draws = jax.random.uniform(jax.random.fold_in(jax.random.fold_in(rng, 6), dim), (blocks,), jnp.float32, low / len(cuts), top_value / len(cuts))
        gain = gain * jnp.repeat(jnp.exp(draws), shape[dim] // blocks).reshape((-1,) + (1,) * (len(shape) - 1 - dim))
    return gain


def centred(rng, extent, spread, bound, cuts=(), held_as=jnp.bfloat16):
    result = spread * jax.random.normal(rng, extent, jnp.float32)
    if cuts:
        result = result * levels(rng, extent, cuts, -0.22, 0.18)
    return jnp.clip(result, -bound, bound).astype(held_as)


def setup_inputs(seed: int = 0) -> dict:
    streams_of = jax.random.split(jax.random.key(seed), 7)
    return {
        "queries": centred(streams_of[0], (TOKENS, HEADS * HEAD_DIM), 1.0, 6.0, ((0, 8), (1, 4))),
        "key_input": centred(streams_of[1], (HOUSE, TOKENS, HEADS * HEAD_DIM), 1.0, 6.0, ((1, 8), (2, 4))),
        "value_input": centred(streams_of[2], (HOUSE, TOKENS, HEADS * HEAD_DIM), 1.0, 6.0, ((1, 8), (2, 4))),
        "beta_rates": draw_beta_rates(jax.random.fold_in(streams_of[6], 71), 0),
        "out_grad": centred(streams_of[4], (TOKENS, D), 0.05, 0.75, ((0, 32),)),
        "out_weight": centred(streams_of[5], (HEADS * HEAD_DIM, D), (HEADS * HEAD_DIM) ** -0.5, 0.09375, ((0, 4),)),
    }


highest = lax.Precision.HIGHEST

def block_solve(key_rows, value_rows, rate_rows):
    length = key_rows.shape[1]
    gram = jnp.einsum('bik,bjk->bij', key_rows, key_rows, precision=highest)
    strict = jnp.tril(jnp.ones((length, length), key_rows.dtype), -1)
    system = jnp.eye(length, dtype=key_rows.dtype) + gram * rate_rows[:, None, :] * strict
    joined = jnp.concatenate([key_rows, value_rows], axis=2)
    solved = jax.scipy.linalg.solve_triangular(system, joined, lower=True, unit_diagonal=True)
    return (solved[..., :key_rows.shape[2]], solved[..., key_rows.shape[2]:])

def read_mask(query_rows, length, dtype):
    house_count = length // query_rows
    upper = house_count * (jnp.arange(query_rows) + 1)
    return (jnp.arange(length)[None, :] < upper[:, None]).astype(dtype)

def block_step(state_in, pieces):
    query_rows, key_rows, value_rows, rate_rows = pieces
    solved_k, solved_v = block_solve(key_rows, value_rows, rate_rows)
    errors = jnp.einsum('bik,bkv->biv', solved_k, state_in, precision=highest) - solved_v
    weighted = errors * rate_rows[:, :, None]
    scores = jnp.einsum('btk,bik->bti', query_rows, key_rows, precision=highest)
    scores = scores * read_mask(query_rows.shape[1], key_rows.shape[1], scores.dtype)[None]
    outputs = jnp.einsum('btk,bkv->btv', query_rows, state_in, precision=highest)
    outputs = outputs - jnp.einsum('bti,biv->btv', scores, weighted, precision=highest)
    state_out = state_in - jnp.einsum('bik,biv->bkv', key_rows, weighted, precision=highest)
    return (state_out, outputs)

def arrange(query_all, raw_keys, value_all, rate_all, block_len):
    tokens, head_count, head_width = query_all.shape
    house_count = raw_keys.shape[0]
    scaling = lax.rsqrt(lax.optimization_barrier(jnp.sum(raw_keys * raw_keys, axis=-1, keepdims=True)) + 1e-06)
    normed = raw_keys * scaling
    blocks = tokens // block_len
    query_blocks = query_all.reshape(blocks, block_len, head_count, head_width).transpose(0, 2, 1, 3)

    def reorder(tensor):
        last_width = tensor.shape[-1]
        shaped = tensor.reshape(house_count, blocks, block_len, head_count, last_width)
        return shaped.transpose(1, 3, 2, 0, 4).reshape(blocks, head_count, block_len * house_count, last_width)
    rate_blocks = rate_all.reshape(head_count, house_count, blocks, block_len)
    rate_blocks = rate_blocks.transpose(2, 0, 3, 1).reshape(blocks, head_count, block_len * house_count)
    return (query_blocks, reorder(normed), reorder(value_all), rate_blocks)

def run_blocks(state_in, query_all, raw_keys, value_all, rate_all, block_len):
    tokens, head_count, head_width = query_all.shape
    pieces = arrange(query_all * head_width ** (-0.5), raw_keys, value_all, rate_all, block_len)
    final, outputs_all = lax.scan(jax.checkpoint(block_step), state_in, pieces)
    return (outputs_all.transpose(0, 2, 1, 3).reshape(tokens, head_count, -1), final)

def reference(queries, key_input, value_input, beta_rates, out_grad, out_weight):
    d_attn = lax.dot_general(out_grad.astype(jnp.float32), out_weight.astype(jnp.float32), (((1,), (1,)), ((), ())), preferred_element_type=jnp.float32).astype(jnp.bfloat16)
    tokens = queries.shape[0]
    query_all = queries.astype(jnp.float32).reshape(tokens, HEADS, HEAD_DIM)
    raw_keys = key_input.astype(jnp.float32).reshape(HOUSE, tokens, HEADS, HEAD_DIM)
    value_all = value_input.astype(jnp.float32).reshape(HOUSE, tokens, HEADS, HEAD_DIM)
    start = jnp.zeros((HEADS, HEAD_DIM, HEAD_DIM), jnp.float32)

    def forward(query_arg, key_arg, value_arg, rate_arg):
        return run_blocks(start, query_arg, key_arg, value_arg, rate_arg, BLOCK)[0]
    outputs_all, pullback = jax.vjp(forward, query_all, raw_keys, value_all, beta_rates)
    grad_q, grad_k, grad_v, grad_b = pullback(d_attn.astype(jnp.float32).reshape(tokens, HEADS, HEAD_DIM))
    return (grad_q.reshape(tokens, HEADS * HEAD_DIM).astype(jnp.bfloat16), grad_k.reshape(HOUSE, tokens, HEADS * HEAD_DIM).astype(jnp.bfloat16), grad_v.reshape(HOUSE, tokens, HEADS * HEAD_DIM).astype(jnp.bfloat16), grad_b)
```

```python
import functools

import jax
import jax.numpy as jnp
from jax import lax
from jax.experimental import pallas as pl
from jax.experimental.pallas import tpu as pltpu
from jax.sharding import PartitionSpec as P

HEAD_DIM = 128
MESH = pl.DeviceIdType.MESH
F32 = jnp.float32
BF16 = jnp.bfloat16


def product(left, right, over_left, over_right, passes=1):
    def one(a, b):
        return lax.dot_general(
            a, b, (((over_left,), (over_right,)), ((), ())), preferred_element_type=F32
        )

    left_high, right_high = left.astype(BF16), right.astype(BF16)
    if passes == 1:
        return one(left_high, right_high)
    total = one(left_high, right_high)
    if left.dtype == F32:
        total += one((left - left_high.astype(F32)).astype(BF16), right_high)
    if right.dtype == F32:
        total += one(left_high, (right - right_high.astype(F32)).astype(BF16))
    return total


def order(shape, axis, tokens, house):
    index = lax.broadcasted_iota(jnp.int32, shape, axis)
    return house * (index % tokens) + index // tokens


def inverse(strict_system, tokens, house, passes):
    shape = strict_system.shape
    row, column = order(shape, 0, tokens, house), order(shape, 1, tokens, house)
    result = jnp.where(row == column, 1.0, 0.0).astype(F32)
    size = 1
    while size < shape[0]:
        joins = (row // (2 * size) == column // (2 * size)) & (row // size != column // size)
        corner = jnp.where(joins, strict_system, 0.0)
        if size == 1:
            result = result - corner
        else:
            half = product(corner, result, 1, 0, passes)
            result = result - product(result, half, 1, 0, passes)
        size *= 2
    return result


def normalize(raw):
    raw = raw.astype(F32)
    scaling = lax.rsqrt(jnp.sum(raw * raw, axis=-1, keepdims=True) + 1e-06)
    return raw * scaling, scaling


def read_mask(tokens, rows):
    reader = lax.broadcasted_iota(jnp.int32, (tokens, rows), 0)
    return lax.broadcasted_iota(jnp.int32, (tokens, rows), 1) % tokens <= reader


def solve_part(query, raw, value, rate, house, inv_passes=3, passes=3):
    tokens = query.shape[0]
    rows = raw.shape[0]
    query = query.astype(F32) * HEAD_DIM ** (-0.5)
    key, _ = normalize(raw)
    gram = product(key, key, 1, 1, inv_passes)
    shape = (rows, rows)
    before = order(shape, 1, tokens, house) < order(shape, 0, tokens, house)
    gram = jnp.where(before, gram, 0.0)
    solver = inverse(gram * rate, tokens, house, inv_passes)
    solved_k = product(solver, key * rate, 1, 0, passes)
    solved_v = product(solver, value.astype(F32) * rate, 1, 0, passes)
    decay = product(key, solved_k, 0, 0, passes)
    offset = product(key, solved_v, 0, 0, passes)
    scores = jnp.where(read_mask(tokens, rows), product(query, key, 1, 1, passes), 0.0)
    reading = query - product(scores, solved_k, 1, 0, passes)
    return gram, solver, solved_k, solved_v, decay, offset, scores, reading


def final_part(
    query, raw, value, rate, gram, solver, solved_k, solved_v, scores, grad, state, adjoint, passes=3
):
    house = raw.shape[0] // query.shape[0]
    tokens = query.shape[0]
    rows = raw.shape[0]
    query = query.astype(F32) * HEAD_DIM ** (-0.5)
    key, scaling = normalize(raw)
    weighted = product(solved_k, state, 1, 0, passes) - solved_v
    errors = product(key, state, 1, 0, passes) - value.astype(F32)
    errors = errors - product(gram, weighted, 1, 0, passes)
    grad_weighted = -product(scores, grad, 0, 0, passes) - product(key, adjoint, 1, 0, passes)
    unscaled = product(solver, grad_weighted, 0, 0, passes)
    pulled = unscaled * rate
    grad_rate = jnp.sum(errors * unscaled, axis=1, keepdims=True)
    grad_scores = -jnp.where(read_mask(tokens, rows), product(grad, weighted, 1, 1, passes), 0.0)
    grad_query = product(grad, state, 1, 1, passes) + product(grad_scores, key, 1, 0, passes)
    shape = (rows, rows)
    before = order(shape, 1, tokens, house) < order(shape, 0, tokens, house)
    grad_gram = -jnp.where(before, product(pulled, weighted, 1, 1, passes), 0.0)
    grad_key = (
        product(grad_scores, query, 0, 0, passes)
        - product(weighted, adjoint, 1, 1, passes)
        + product(pulled, state, 1, 1, passes)
        + product(grad_gram, key, 1, 0, passes)
        + product(grad_gram, key, 0, 0, passes)
    )
    along = jnp.sum(grad_key * key, axis=1, keepdims=True)
    grad_raw = scaling * (grad_key - key * along)
    return grad_query * HEAD_DIM ** (-0.5), grad_raw, -pulled, grad_rate


def kernel(
    ctx_count,
    head_count,
    query_ref, raw_ref, value_ref, rate_ref, grad_ref, weight_ref,
    out_query, out_key, out_value, out_rate,
    weight, gathered, rates, grad_rates, grads,
    gram, solver, solved_k, solved_v, decay, offset, scores, reading, local_grad,
    state, state_out, adjoint, adjoint_out,
    weight_sem, up_send, down_send, gather_recv, state_send, state_recv, adjoint_send, adjoint_recv,
):
    me, column = lax.axis_index("ctx"), lax.axis_index("head")
    house, tokens = raw_ref.shape[0], raw_ref.shape[1]
    heads = state.shape[0]
    shard = grad_ref.shape[0]
    rows = house * tokens

    weight_copy = pltpu.make_async_copy(weight_ref, weight, weight_sem)
    weight_copy.start()

    barrier = pltpu.get_barrier_semaphore()
    neighbours = (
        (me > 0, {"ctx": me - 1}),
        (me < ctx_count - 1, {"ctx": me + 1}),
        (column > 0, {"head": column - 1}),
        (column < head_count - 1, {"head": column + 1}),
    )
    for there, device in neighbours:
        @pl.when(there)
        def _():
            pl.semaphore_signal(barrier, inc=1, device_id=device, device_id_type=MESH)
    pl.semaphore_wait(barrier, sum(there.astype(jnp.int32) for there, _ in neighbours))

    def slot(owner):
        return gathered.at[pl.ds(pl.multiple_of(owner * shard, shard), shard)]

    def passing(owner, up):
        return pltpu.make_async_remote_copy(
            src_ref=slot(owner),
            dst_ref=slot(owner),
            send_sem=(up_send if up else down_send).at[owner],
            recv_sem=gather_recv.at[owner],
            device_id={"head": lax.rem(column + (1 if up else head_count - 1), head_count)},
            device_id_type=MESH,
        )

    gathered[pl.ds(pl.multiple_of(column * shard, shard), shard)] = grad_ref[...]

    def send_on(owner, up):
        @pl.when(column < head_count - 1 if up else column > 0)
        def _():
            passing(owner, up).start()

    send_on(column, True)
    send_on(column, False)

    rates[...] = jnp.zeros_like(rates)
    grad_rates[...] = jnp.zeros_like(grad_rates)
    rates[pl.ds(0, house * heads)] = rate_ref[...]
    rates[...] = jnp.transpose(rates[...])

    lanes = lax.broadcasted_iota(jnp.int32, (tokens, tokens), 1)

    def rate_of(head):
        parts = [
            jnp.sum(jnp.where(lanes == head * house + j, rates[...], 0.0), axis=1, keepdims=True)
            for j in range(house)
        ]
        return jnp.concatenate(parts, axis=0)

    def columns(head):
        return pl.ds(pl.multiple_of(head * HEAD_DIM, HEAD_DIM), HEAD_DIM)

    def load(ref, head):
        return ref[:, :, columns(head)].reshape(rows, HEAD_DIM)

    def solve_head(head):
        results = solve_part(
            query_ref[:, columns(head)], load(raw_ref, head), load(value_ref, head), rate_of(head), house
        )
        kept = (gram, solver, solved_k, solved_v, decay, offset, scores, reading)
        for ref, result in zip(kept, results):
            ref[head] = result.astype(ref.dtype)

    together = 2 if heads % 2 == 0 else 1
    turns = heads // together

    def gather_turn(turn):
        for owner, up in ((column - turn, True), (column + turn, False)):
            @pl.when((owner >= 0) & (owner < head_count))
            def _():
                passing(owner, up).wait_recv()
                send_on(owner, up)

    def solve_turn(turn, carry):
        for part in range(together):
            solve_head(turn * together + part)

        @pl.when((turn + 1) < head_count)
        def _():
            gather_turn(turn + 1)

        return carry

    lax.fori_loop(0, turns, solve_turn, 0)
    for turn in range(turns + 1, head_count):
        gather_turn(turn)

    @pl.when(me == 0)
    def _():
        state[...] = jnp.zeros_like(state)

    @pl.when(me == ctx_count - 1)
    def _():
        adjoint[...] = jnp.zeros_like(adjoint)

    weight_copy.wait()

    def grad_turn(turn, carry):
        part = pl.ds(pl.multiple_of(turn * together * HEAD_DIM, HEAD_DIM), together * HEAD_DIM)
        block = product(gathered[...], weight[part, :], 1, 1).astype(BF16)
        for index in range(together):
            head = turn * together + index
            grad = block[:, index * HEAD_DIM : (index + 1) * HEAD_DIM]
            grads[head] = grad
            local_grad[head] = product(reading[head], grad, 0, 0)
        return carry

    lax.fori_loop(0, turns, grad_turn, 0)

    def state_copy(head):
        return pltpu.make_async_remote_copy(
            src_ref=state_out.at[head], dst_ref=state.at[head],
            send_sem=state_send.at[head], recv_sem=state_recv.at[head],
            device_id={"ctx": lax.rem(me + 1, ctx_count)}, device_id_type=MESH,
        )

    def adjoint_copy(head):
        return pltpu.make_async_remote_copy(
            src_ref=adjoint_out.at[head], dst_ref=adjoint.at[head],
            send_sem=adjoint_send.at[head], recv_sem=adjoint_recv.at[head],
            device_id={"ctx": lax.rem(me + ctx_count - 1, ctx_count)}, device_id_type=MESH,
        )

    far = ctx_count - 1 - me

    def wave(step, carry):
        head_f = step - me

        @pl.when((head_f >= 0) & (head_f < heads))
        def _():
            @pl.when(me > 0)
            def _():
                state_copy(head_f).wait_recv()

            @pl.when(far > 0)
            def _():
                held = state[head_f]
                state_out[head_f] = held + offset[head_f] - product(decay[head_f], held, 1, 0)
                state_copy(head_f).start()

        head_b = step - far

        @pl.when((head_b >= 0) & (head_b < heads))
        def _():
            @pl.when(far > 0)
            def _():
                adjoint_copy(head_b).wait_recv()

            @pl.when(me > 0)
            def _():
                held = adjoint[head_b]
                adjoint_out[head_b] = held + local_grad[head_b] - product(decay[head_b], held, 0, 0)
                adjoint_copy(head_b).start()

        head = step - jnp.maximum(me, far)

        @pl.when((head >= 0) & (head < heads))
        def _():
            grad_query, grad_raw, grad_value, grad_rate = final_part(
                query_ref[:, columns(head)], load(raw_ref, head), load(value_ref, head), rate_of(head),
                gram[head], solver[head], solved_k[head], solved_v[head], scores[head],
                grads[head], state[head], adjoint[head],
            )
            out_query[:, columns(head)] = grad_query.astype(BF16)
            out_key[:, :, columns(head)] = grad_raw.reshape(house, tokens, HEAD_DIM).astype(BF16)
            out_value[:, :, columns(head)] = grad_value.reshape(house, tokens, HEAD_DIM).astype(BF16)
            total = grad_rates[...]
            for j in range(house):
                total = jnp.where(
                    lanes == head * house + j, grad_rate[j * tokens : (j + 1) * tokens], total
                )
            grad_rates[...] = total

        return carry

    lax.fori_loop(0, ctx_count - 1 + heads, wave, 0)

    out_rate[...] = jnp.transpose(grad_rates[...])[: house * heads]

    def finish(head, carry):
        @pl.when(far > 0)
        def _():
            state_copy(head).wait_send()

        @pl.when(me > 0)
        def _():
            adjoint_copy(head).wait_send()

        return carry

    lax.fori_loop(0, heads, finish, 0)
    for owner in range(head_count):
        @pl.when((owner <= column) & (column < head_count - 1))
        def _():
            passing(owner, True).wait_send()

        @pl.when((owner >= column) & (column > 0))
        def _():
            passing(owner, False).wait_send()


def shards(queries, key_input, value_input, beta_rates, out_grad, out_weight):
    house, tokens, width = key_input.shape
    heads = width // HEAD_DIM
    rows = house * tokens
    ctx_count, head_count = lax.axis_size("ctx"), lax.axis_size("head")
    vmem = pl.BlockSpec(memory_space=pltpu.VMEM)

    def held(*shape, dtype=F32):
        return pltpu.VMEM((heads,) + shape, dtype)

    results = pl.pallas_call(
        functools.partial(kernel, ctx_count, head_count),
        out_shape=(
            jax.ShapeDtypeStruct(queries.shape, BF16),
            jax.ShapeDtypeStruct(key_input.shape, BF16),
            jax.ShapeDtypeStruct(value_input.shape, BF16),
            jax.ShapeDtypeStruct((heads * house, tokens), F32),
        ),
        in_specs=[vmem] * 5 + [pl.BlockSpec(memory_space=pl.ANY)],
        out_specs=(vmem,) * 4,
        scratch_shapes=[
            pltpu.VMEM(out_weight.shape, BF16),
            pltpu.VMEM((tokens, out_grad.shape[1]), BF16),
            pltpu.VMEM((tokens, tokens), F32),
            pltpu.VMEM((tokens, tokens), F32),
            held(tokens, HEAD_DIM, dtype=BF16),
            held(rows, rows, dtype=BF16),
            held(rows, rows, dtype=BF16),
            held(rows, HEAD_DIM),
            held(rows, HEAD_DIM),
            held(HEAD_DIM, HEAD_DIM, dtype=BF16),
            held(HEAD_DIM, HEAD_DIM),
            held(tokens, rows, dtype=BF16),
            held(tokens, HEAD_DIM, dtype=BF16),
            held(HEAD_DIM, HEAD_DIM),
            held(HEAD_DIM, HEAD_DIM),
            held(HEAD_DIM, HEAD_DIM),
            held(HEAD_DIM, HEAD_DIM),
            held(HEAD_DIM, HEAD_DIM),
            pltpu.SemaphoreType.DMA,
            pltpu.SemaphoreType.DMA((head_count,)),
            pltpu.SemaphoreType.DMA((head_count,)),
            pltpu.SemaphoreType.DMA((head_count,)),
            pltpu.SemaphoreType.DMA((heads,)),
            pltpu.SemaphoreType.DMA((heads,)),
            pltpu.SemaphoreType.DMA((heads,)),
            pltpu.SemaphoreType.DMA((heads,)),
        ],
        compiler_params=pltpu.CompilerParams(
            collective_id=0, has_side_effects=True, vmem_limit_bytes=56 * 1024 * 1024
        ),
    )(
        queries,
        key_input,
        value_input,
        beta_rates.reshape(heads * house, tokens),
        out_grad,
        out_weight,
    )
    return results[:3] + (results[3].reshape(beta_rates.shape),)


def solution(mesh):
    placed = (
        P("ctx", "head"),
        P(None, "ctx", "head"),
        P(None, "ctx", "head"),
        P("head", None, "ctx"),
        P(("ctx", "head"), None),
        P("head", None),
    )
    return jax.shard_map(
        shards,
        mesh=mesh,
        in_specs=placed,
        out_specs=placed[:4],
        check_vma=False,
    )
```

```python
import functools

import jax
import jax.numpy as jnp
from jax import lax
from jax.experimental import pallas as pl
from jax.experimental.pallas import tpu as pltpu
from jax.sharding import PartitionSpec as P

HEAD_DIM = 128
MESH = pl.DeviceIdType.MESH
F32 = jnp.float32
BF16 = jnp.bfloat16
SOLVER = BF16
SPLIT = {
    "gram": "lr", "inv1": "lr", "inv2": "lr", "sk": "lr", "sv": "lr", "dec": "lr", "off": "lr", "sc": "lr", "rd": "lr", "w": "lr",
    "gw1": "lr", "gs": "lr", "q2": "lr", "k1": "lr", "gw2": "lr", "un": "lr", "gg": "lr", "k2": "lr", "k4": "lr",
}


def product(left, right, over_left, over_right, split=""):
    def one(a, b):
        return lax.dot_general(
            a, b, (((over_left,), (over_right,)), ((), ())), preferred_element_type=F32
        )

    left_high, right_high = left.astype(BF16), right.astype(BF16)
    total = one(left_high, right_high)
    if "l" in split and left.dtype == F32:
        total += one((left - left_high.astype(F32)).astype(BF16), right_high)
    if "r" in split and right.dtype == F32:
        total += one(left_high, (right - right_high.astype(F32)).astype(BF16))
    return total


def order(shape, axis, tokens, house):
    index = lax.broadcasted_iota(jnp.int32, shape, axis)
    return house * (index % tokens) + index // tokens


def inverse(strict_system, tokens, house):
    shape = strict_system.shape
    row, column = order(shape, 0, tokens, house), order(shape, 1, tokens, house)
    result = jnp.where(row == column, 1.0, 0.0).astype(F32)
    size = 1
    while size < shape[0]:
        joins = (row // (2 * size) == column // (2 * size)) & (row // size != column // size)
        corner = jnp.where(joins, strict_system, 0.0)
        if size == 1:
            result = result - corner
        else:
            half = product(corner, result, 1, 0, SPLIT["inv1"])
            result = result - product(result, half, 1, 0, SPLIT["inv2"])
        size *= 2
    return result


def normalize(raw):
    raw = raw.astype(F32)
    scaling = lax.rsqrt(jnp.sum(raw * raw, axis=-1, keepdims=True) + 1e-06)
    return raw * scaling, scaling


def read_mask(tokens, rows):
    reader = lax.broadcasted_iota(jnp.int32, (tokens, rows), 0)
    return lax.broadcasted_iota(jnp.int32, (tokens, rows), 1) % tokens <= reader


def strict_mask(tokens, house):
    shape = (house * tokens, house * tokens)
    return order(shape, 1, tokens, house) < order(shape, 0, tokens, house)


def solve_part(query, raw, value, rate, house):
    tokens = query.shape[0]
    query = query.astype(F32) * HEAD_DIM ** (-0.5)
    key, _ = normalize(raw)
    gram = product(key, key, 1, 1, SPLIT["gram"])
    gram = jnp.where(strict_mask(tokens, house), gram, 0.0)
    solver = inverse(gram * rate, tokens, house)
    solved_k = product(solver, key * rate, 1, 0, SPLIT["sk"])
    solved_v = product(solver, value.astype(F32) * rate, 1, 0, SPLIT["sv"])
    decay = product(key, solved_k, 0, 0, SPLIT["dec"])
    offset = product(key, solved_v, 0, 0, SPLIT["off"])
    scores = jnp.where(read_mask(tokens, gram.shape[0]), product(query, key, 1, 1, SPLIT["sc"]), 0.0)
    reading = query - product(scores, solved_k, 1, 0, SPLIT["rd"])
    return gram, solver, solved_k, solved_v, decay, offset, scores, reading


def early_part(query, raw, value, gram, solved_k, solved_v, scores, grad, state):
    tokens = query.shape[0]
    query = query.astype(F32) * HEAD_DIM ** (-0.5)
    key, _ = normalize(raw)
    weighted = product(solved_k, state, 1, 0, SPLIT["w"]) - solved_v
    errors = product(key, state, 1, 0) - value.astype(F32) - product(gram, weighted, 1, 0)
    grad_weighted = -product(scores, grad, 0, 0, SPLIT["gw1"])
    grad_scores = product(grad, weighted, 1, 1, SPLIT["gs"])
    grad_scores = jnp.where(read_mask(tokens, raw.shape[0]), -grad_scores, 0.0)
    grad_query = product(grad, state, 1, 1, "r") + product(grad_scores, key, 1, 0, SPLIT["q2"])
    grad_key = product(grad_scores, query, 0, 0, SPLIT["k1"])
    return weighted, errors, grad_weighted, grad_query * HEAD_DIM ** (-0.5), grad_key


def late_part(raw, rate, solver, weighted, errors, grad_weighted, grad_key, state, adjoint, house):
    tokens = raw.shape[0] // house
    key, scaling = normalize(raw)
    grad_weighted = grad_weighted - product(key, adjoint, 1, 0, SPLIT["gw2"])
    unscaled = product(solver, grad_weighted, 0, 0, SPLIT["un"])
    pulled = unscaled * rate
    grad_rate = jnp.sum(errors * unscaled, axis=1, keepdims=True)
    grad_gram = -jnp.where(strict_mask(tokens, house), product(pulled, weighted, 1, 1, SPLIT["gg"]), 0.0)
    grad_key = (
        grad_key
        - product(weighted, adjoint, 1, 1, SPLIT["k2"])
        + product(pulled, state, 1, 1, SPLIT["k2"])
        + product(grad_gram, key, 1, 0, SPLIT["k4"])
        + product(grad_gram, key, 0, 0, SPLIT["k4"])
    )
    along = jnp.sum(grad_key * key, axis=1, keepdims=True)
    grad_raw = scaling * (grad_key - key * along)
    return grad_raw, -pulled, grad_rate


def kernel(
    ctx_count,
    head_count,
    query_ref, raw_ref, value_ref, rate_ref, grad_ref, weight_ref,
    out_query, out_key, out_value, out_rate,
    weight, gathered, rates, grads,
    gram, solver, solved_k, solved_v, decay, offset, scores, reading, local_grad,
    errors, grad_weighted, grad_key, state, adjoint,
    decay_in, offset_in, grad_in, states, adjoints,
    weight_sem, up_send, down_send, gather_recv,
    decay_send, decay_recv, offset_send, offset_recv, grad_send, grad_recv,
    state_send, state_recv, adjoint_send, adjoint_recv,
):
    me, column = lax.axis_index("ctx"), lax.axis_index("head")
    house, tokens = raw_ref.shape[0], raw_ref.shape[1]
    heads = state.shape[0]
    shard = grad_ref.shape[0]
    rows = house * tokens
    spacing = ctx_count // heads
    owns = lax.rem(me, spacing) == 0
    mine = me // spacing

    weight_copy = pltpu.make_async_copy(weight_ref, weight, weight_sem)
    weight_copy.start()

    barrier = pltpu.get_barrier_semaphore()

    def greet(there, device):
        @pl.when(there)
        def _():
            pl.semaphore_signal(barrier, inc=1, device_id=device, device_id_type=MESH)

        return there.astype(jnp.int32)

    peers = greet(column > 0, {"head": column - 1})
    peers += greet(column < head_count - 1, {"head": column + 1})
    for other in range(ctx_count):
        meets = (me != other) if other % spacing == 0 else (me != other) & owns
        peers += greet(meets, {"ctx": other})
    pl.semaphore_wait(barrier, peers)

    def slot(owner):
        return gathered.at[pl.ds(pl.multiple_of(owner * shard, shard), shard)]

    def passing(owner, up):
        return pltpu.make_async_remote_copy(
            src_ref=slot(owner),
            dst_ref=slot(owner),
            send_sem=(up_send if up else down_send).at[owner],
            recv_sem=gather_recv.at[owner],
            device_id={"head": lax.rem(column + (1 if up else head_count - 1), head_count)},
            device_id_type=MESH,
        )

    gathered[pl.ds(pl.multiple_of(column * shard, shard), shard)] = grad_ref[...]

    def send_on(owner, up):
        @pl.when(column < head_count - 1 if up else column > 0)
        def _():
            passing(owner, up).start()

    send_on(column, True)
    send_on(column, False)

    rates[...] = jnp.zeros_like(rates)
    rates[pl.ds(0, house * heads)] = rate_ref[...]
    rates[...] = jnp.transpose(rates[...])

    lanes = lax.broadcasted_iota(jnp.int32, (tokens, tokens), 1)

    def rate_of(head):
        parts = [
            jnp.sum(jnp.where(lanes == head * house + j, rates[...], 0.0), axis=1, keepdims=True)
            for j in range(house)
        ]
        return jnp.concatenate(parts, axis=0)

    def columns(head):
        return pl.ds(pl.multiple_of(head * HEAD_DIM, HEAD_DIM), HEAD_DIM)

    def load(ref, head):
        return ref[:, :, columns(head)].reshape(rows, HEAD_DIM)

    def to_owner(kept, landing, send, recv, head, source):
        return pltpu.make_async_remote_copy(
            src_ref=kept.at[head], dst_ref=landing.at[source], send_sem=send.at[head],
            recv_sem=recv.at[source], device_id={"ctx": head * spacing}, device_id_type=MESH,
        )

    def give(kept, landing, send, recv, head):
        away = me != head * spacing

        @pl.when(away)
        def _():
            to_owner(kept, landing, send, recv, head, me).start()

        @pl.when(jnp.logical_not(away))
        def _():
            landing[me] = kept[head]

    decay_args = (decay, decay_in, decay_send, decay_recv)
    offset_args = (offset, offset_in, offset_send, offset_recv)
    grad_args = (local_grad, grad_in, grad_send, grad_recv)

    def to_user(made, landing, send, recv, user, head):
        return pltpu.make_async_remote_copy(
            src_ref=made.at[user], dst_ref=landing.at[head], send_sem=send.at[user],
            recv_sem=recv.at[head], device_id={"ctx": user}, device_id_type=MESH,
        )

    def hand_out(made, landing, send, recv, user):
        @pl.when(me != user)
        def _():
            to_user(made, landing, send, recv, user, mine).start()

        @pl.when(me == user)
        def _():
            landing[mine] = made[user]

    state_args = (states, state, state_send, state_recv)
    adjoint_args = (adjoints, adjoint, adjoint_send, adjoint_recv)

    def solve_head(head):
        results = solve_part(
            query_ref[:, columns(head)], load(raw_ref, head), load(value_ref, head), rate_of(head), house
        )
        kept = (gram, solver, solved_k, solved_v, decay, offset, scores, reading)
        for ref, result in zip(kept, results):
            ref[head] = result.astype(ref.dtype)

    together = 2 if heads % 2 == 0 else 1
    turns = heads // together

    def gather_turn(turn):
        for owner, up in ((column - turn, True), (column + turn, False)):
            @pl.when((owner >= 0) & (owner < head_count))
            def _():
                passing(owner, up).wait_recv()
                send_on(owner, up)

    def solve_turn(turn, carry):
        for part in range(together):
            solve_head(turn * together + part)
        for part in range(together):
            give(*decay_args, turn * together + part)
            give(*offset_args, turn * together + part)

        @pl.when((turn + 1) < head_count)
        def _():
            gather_turn(turn + 1)

        return carry

    lax.fori_loop(0, turns, solve_turn, 0)
    for turn in range(turns + 1, head_count):
        gather_turn(turn)

    weight_copy.wait()

    def grad_turn(turn, carry):
        part = pl.ds(pl.multiple_of(turn * together * HEAD_DIM, HEAD_DIM), together * HEAD_DIM)
        block = product(gathered[...], weight[part, :], 1, 1).astype(BF16)
        for index in range(together):
            head = turn * together + index
            grad = block[:, index * HEAD_DIM : (index + 1) * HEAD_DIM]
            grads[head] = grad
            local_grad[head] = product(reading[head], grad, 0, 0)
            give(*grad_args, head)
        return carry

    lax.fori_loop(0, turns, grad_turn, 0)

    @pl.when(owns)
    def _():
        def arrive(args, source):
            @pl.when(me != source)
            def _():
                to_owner(*args, mine, source).wait_recv()

        def forward(user, held):
            states[user] = held
            hand_out(*state_args, user)
            arrive(decay_args, user)
            arrive(offset_args, user)
            return held + offset_in[user] - product(decay_in[user], held, 1, 0)

        zero = jnp.zeros((HEAD_DIM, HEAD_DIM), F32)
        lax.fori_loop(0, ctx_count, forward, zero)

        def backward(step, held):
            user = ctx_count - 1 - step
            adjoints[user] = held
            hand_out(*adjoint_args, user)
            arrive(grad_args, user)
            return held + grad_in[user] - product(decay_in[user], held, 0, 0)

        lax.fori_loop(0, ctx_count, backward, zero)

    def early_head(head):
        @pl.when(me != head * spacing)
        def _():
            to_user(*state_args, me, head).wait_recv()

    def early_turn(turn, carry):
        for part in range(together):
            early_head(turn * together + part)
        for part in range(together):
            head = turn * together + part
            results = early_part(
                query_ref[:, columns(head)], load(raw_ref, head), load(value_ref, head), gram[head],
                solved_k[head], solved_v[head], scores[head], grads[head], state[head],
            )
            solved_v[head], errors[head], grad_weighted[head] = results[:3]
            out_query[:, columns(head)] = results[3].astype(BF16)
            grad_key[head] = results[4]
        return carry

    lax.fori_loop(0, turns, early_turn, 0)

    def late_turn(turn, total):
        for part in range(together):
            head = turn * together + part

            @pl.when(me != head * spacing)
            def _():
                to_user(*adjoint_args, me, head).wait_recv()

        for part in range(together):
            head = turn * together + part
            grad_raw, grad_value, grad_rate = late_part(
                load(raw_ref, head), rate_of(head), solver[head], solved_v[head], errors[head],
                grad_weighted[head], grad_key[head], state[head], adjoint[head], house,
            )
            out_key[:, :, columns(head)] = grad_raw.reshape(house, tokens, HEAD_DIM).astype(BF16)
            out_value[:, :, columns(head)] = grad_value.reshape(house, tokens, HEAD_DIM).astype(BF16)
            for j in range(house):
                total = jnp.where(
                    lanes == head * house + j, grad_rate[j * tokens : (j + 1) * tokens], total
                )
        return total

    total = lax.fori_loop(0, turns, late_turn, jnp.zeros((tokens, tokens), F32))
    out_rate[...] = jnp.transpose(total)[: house * heads]

    def given(head, carry):
        @pl.when(me != head * spacing)
        def _():
            for args in (decay_args, offset_args, grad_args):
                to_owner(*args, head, me).wait_send()

        return carry

    lax.fori_loop(0, heads, given, 0)

    def handed(user, carry):
        @pl.when(owns & (me != user))
        def _():
            for args in (state_args, adjoint_args):
                to_user(*args, user, mine).wait_send()

        return carry

    lax.fori_loop(0, ctx_count, handed, 0)
    for owner in range(head_count):
        @pl.when((owner <= column) & (column < head_count - 1))
        def _():
            passing(owner, True).wait_send()

        @pl.when((owner >= column) & (column > 0))
        def _():
            passing(owner, False).wait_send()


def shards(queries, key_input, value_input, beta_rates, out_grad, out_weight):
    house, tokens, width = key_input.shape
    heads = width // HEAD_DIM
    rows = house * tokens
    square = (HEAD_DIM, HEAD_DIM)
    ctx_count, head_count = lax.axis_size("ctx"), lax.axis_size("head")
    vmem = pl.BlockSpec(memory_space=pltpu.VMEM)

    def held(*shape, dtype=F32):
        return pltpu.VMEM((heads,) + shape, dtype)

    results = pl.pallas_call(
        functools.partial(kernel, ctx_count, head_count),
        out_shape=(
            jax.ShapeDtypeStruct(queries.shape, BF16),
            jax.ShapeDtypeStruct(key_input.shape, BF16),
            jax.ShapeDtypeStruct(value_input.shape, BF16),
            jax.ShapeDtypeStruct((heads * house, tokens), F32),
        ),
        in_specs=[vmem] * 5 + [pl.BlockSpec(memory_space=pl.ANY)],
        out_specs=(vmem,) * 4,
        scratch_shapes=[
            pltpu.VMEM(out_weight.shape, BF16),
            pltpu.VMEM((tokens, out_grad.shape[1]), BF16),
            pltpu.VMEM((tokens, tokens), F32),
            held(tokens, HEAD_DIM, dtype=BF16),
            held(rows, rows, dtype=BF16),
            held(rows, rows, dtype=SOLVER),
            held(rows, HEAD_DIM),
            held(rows, HEAD_DIM),
            held(*square, dtype=BF16),
            held(*square),
            held(tokens, rows, dtype=BF16),
            held(tokens, HEAD_DIM, dtype=BF16),
            held(*square),
            held(rows, HEAD_DIM),
            held(rows, HEAD_DIM),
            held(rows, HEAD_DIM),
            held(*square),
            held(*square),
            pltpu.VMEM((ctx_count,) + square, BF16),
            pltpu.VMEM((ctx_count,) + square, F32),
            pltpu.VMEM((ctx_count,) + square, F32),
            pltpu.VMEM((ctx_count,) + square, F32),
            pltpu.VMEM((ctx_count,) + square, F32),
            pltpu.SemaphoreType.DMA,
        ]
        + [
            pltpu.SemaphoreType.DMA((count,))
            for count in (head_count,) * 3 + (heads, ctx_count) * 3 + (ctx_count, heads) * 2
        ],
        compiler_params=pltpu.CompilerParams(
            collective_id=0, has_side_effects=True, vmem_limit_bytes=56 * 1024 * 1024
        ),
    )(
        queries,
        key_input,
        value_input,
        beta_rates.reshape(heads * house, tokens),
        out_grad,
        out_weight,
    )
    return results[:3] + (results[3].reshape(beta_rates.shape),)


def solution(mesh):
    placed = (
        P("ctx", "head"),
        P(None, "ctx", "head"),
        P(None, "ctx", "head"),
        P("head", None, "ctx"),
        P(("ctx", "head"), None),
        P("head", None),
    )
    return jax.shard_map(
        shards,
        mesh=mesh,
        in_specs=placed,
        out_specs=placed[:4],
        check_vma=False,
    )
```

```python
import functools

import jax
import jax.numpy as jnp
from jax import lax
from jax.experimental import pallas as pl
from jax.experimental.pallas import tpu as pltpu
from jax.sharding import PartitionSpec as P

HEAD_DIM = 128
MESH = pl.DeviceIdType.MESH
F32 = jnp.float32
BF16 = jnp.bfloat16
SOLVER = BF16
SPLIT = {
    "inv": "lr", "sk": "l", "sv": "l", "maps": "r", "rd": "lr", "w": "", "gs": "", "q1": "",
    "q2": "", "k1": "", "gw2": "", "un": "r", "gg": "", "k2": "", "k4": "l",
}


def product(left, right, over_left, over_right, split=""):
    def one(a, b):
        return lax.dot_general(
            a, b, (((over_left,), (over_right,)), ((), ())), preferred_element_type=F32
        )

    left_high, right_high = left.astype(BF16), right.astype(BF16)
    total = one(left_high, right_high)
    if "l" in split and left.dtype == F32:
        total += one((left - left_high.astype(F32)).astype(BF16), right_high)
    if "r" in split and right.dtype == F32:
        total += one(left_high, (right - right_high.astype(F32)).astype(BF16))
    return total


def order(shape, axis, tokens, house):
    index = lax.broadcasted_iota(jnp.int32, shape, axis)
    return house * (index % tokens) + index // tokens


def inverse(strict_system, tokens, house):
    shape = strict_system.shape
    rows = shape[0]
    apart = order(shape, 0, tokens, house) ^ order(shape, 1, tokens, house)
    result = -jnp.where(apart == 1, strict_system, 0.0)
    size = 2
    while size < rows:
        corner = jnp.where((apart >= size) & (apart < 2 * size), strict_system, 0.0)
        span = size // house
        if span % 8:
            half = corner + product(corner, result, 1, 0, SPLIT["inv"])
            result = result - half - product(result, half, 1, 0, SPLIT["inv"])
        else:
            pairs = (house, tokens // (2 * span), 2, span, rows)

            def second(array):
                return array.reshape(pairs)[:, :, 1].reshape(rows // 2, rows)

            def joined(first, last):
                parts = [part.reshape(pairs[:2] + (1, span, rows)) for part in (first, last)]
                return jnp.concatenate(parts, axis=2).reshape(shape)

            half = second(corner)
            half = half + product(half, result, 1, 0, SPLIT["inv"])
            lower = second(result)
            whole = joined(jnp.zeros_like(half), half)
            lower = lower - half - product(lower, whole, 1, 0, SPLIT["inv"])
            result = joined(result.reshape(pairs)[:, :, 0].reshape(rows // 2, rows), lower)
        size *= 2
    return result


def scaling_of(raw):
    raw = raw.astype(F32)
    return lax.rsqrt(jnp.sum(raw * raw, axis=-1, keepdims=True) + 1e-06)


def read_mask(tokens, rows):
    reader = lax.broadcasted_iota(jnp.int32, (tokens, rows), 0)
    return lax.broadcasted_iota(jnp.int32, (tokens, rows), 1) % tokens <= reader


def strict_mask(tokens, house):
    shape = (house * tokens, house * tokens)
    return order(shape, 1, tokens, house) < order(shape, 0, tokens, house)


def solve_part(query, raw, value, rate, rate_row, house):
    tokens = query.shape[0]
    rows = raw.shape[0]
    scaling = scaling_of(raw)
    index = [lax.broadcasted_iota(jnp.int32, (rows, rows), axis) for axis in (0, 1)]
    scaling_row = jnp.sum(jnp.where(index[0] == index[1], scaling, 0.0), axis=0, keepdims=True)
    gram = product(raw, raw, 1, 1)
    gram = jnp.where(strict_mask(tokens, house), gram * scaling * scaling_row, 0.0)
    solver = inverse(gram * rate, tokens, house)
    scaled_raw = raw.astype(F32) * (scaling * rate)
    solved_k = scaled_raw + product(solver * (rate_row * scaling_row), raw, 1, 0, SPLIT["sk"])
    solved_v = value.astype(F32) * rate + product(solver * rate_row, value, 1, 0, SPLIT["sv"])
    both = jnp.concatenate([solved_k * scaling, solved_v * scaling], axis=1)
    maps = product(raw, both, 0, 0, SPLIT["maps"])
    scores = product(query, raw, 1, 1) * (scaling_row * HEAD_DIM ** (-0.5))
    scores = jnp.where(read_mask(tokens, rows), scores, 0.0)
    reading = query.astype(F32) * HEAD_DIM ** (-0.5) - product(scores, solved_k, 1, 0, SPLIT["rd"])
    return (
        gram, solver, solved_k, solved_v, maps[:, :HEAD_DIM], maps[:, HEAD_DIM:], scores, reading,
        jnp.broadcast_to(scaling_row, (8, rows)),
    )


def early_part(query, raw, value, gram, solved_k, solved_v, scores, scaling_row, grad, state):
    tokens = query.shape[0]
    weighted = product(solved_k, state, 1, 0, SPLIT["w"]) - solved_v
    errors = product(raw, state, 1, 0) * scaling_of(raw) - value.astype(F32)
    errors = errors - product(gram, weighted, 1, 0)
    grad_weighted = -product(scores, grad, 0, 0)
    grad_scores = -product(grad, weighted, 1, 1, SPLIT["gs"]) * HEAD_DIM ** (-0.5)
    grad_scores = jnp.where(read_mask(tokens, raw.shape[0]), grad_scores, 0.0)
    grad_query = product(grad, state, 1, 1, SPLIT["q1"]) * HEAD_DIM ** (-0.5)
    grad_query = grad_query + product(grad_scores * scaling_row, raw, 1, 0, SPLIT["q2"])
    grad_key = product(grad_scores, query, 0, 0, SPLIT["k1"])
    return weighted, errors, grad_weighted, grad_query, grad_key


def late_part(
    raw, rate, solver, scaling_row, weighted, errors, grad_weighted, grad_key, state, adjoint, house
):
    tokens = raw.shape[0] // house
    scaling = scaling_of(raw)
    key = raw.astype(F32) * scaling
    grad_weighted = grad_weighted - product(raw, adjoint, 1, 0, SPLIT["gw2"]) * scaling
    unscaled = grad_weighted + product(solver, grad_weighted, 0, 0, SPLIT["un"])
    pulled = unscaled * rate
    grad_rate = jnp.sum(errors * unscaled, axis=1, keepdims=True)
    grad_gram = jnp.where(strict_mask(tokens, house), product(pulled, weighted, 1, 1, SPLIT["gg"]), 0.0)
    grad_gram = (grad_gram + jnp.transpose(grad_gram)) * scaling_row
    rows_side = jnp.concatenate([-weighted, pulled], axis=1)
    state_side = jnp.concatenate([adjoint, state], axis=1)
    grad_key = grad_key + product(rows_side, state_side, 1, 1, SPLIT["k2"])
    grad_key = grad_key - product(grad_gram, raw, 1, 0, SPLIT["k4"])
    along = jnp.sum(grad_key * key, axis=1, keepdims=True)
    grad_raw = scaling * (grad_key - key * along)
    return grad_raw, -pulled, grad_rate


def kernel(
    ctx_count,
    head_count,
    query_ref, raw_ref, value_ref, rate_ref, grad_ref, weight_ref,
    out_query, out_key, out_value, out_rate,
    weight, gathered, rates, grads,
    gram, solver, solved_k, solved_v, decay, offset, scores, reading, local_grad,
    scalings, errors, grad_weighted, grad_key, state, adjoint,
    decay_in, offset_in, grad_in, states, adjoints,
    weight_sem, up_send, down_send, gather_recv,
    decay_send, decay_recv, offset_send, offset_recv, grad_send, grad_recv,
    state_send, state_recv, adjoint_send, adjoint_recv,
):
    me, column = lax.axis_index("ctx"), lax.axis_index("head")
    house, tokens = raw_ref.shape[0], raw_ref.shape[1]
    heads = state.shape[0]
    shard = grad_ref.shape[0]
    rows = house * tokens
    spacing = ctx_count // heads
    owns = lax.rem(me, spacing) == 0
    mine = me // spacing

    weight_copy = pltpu.make_async_copy(weight_ref, weight, weight_sem)
    weight_copy.start()

    barrier = pltpu.get_barrier_semaphore()

    def greet(there, device):
        @pl.when(there)
        def _():
            pl.semaphore_signal(barrier, inc=1, device_id=device, device_id_type=MESH)

        return there.astype(jnp.int32)

    peers = greet(column > 0, {"head": column - 1})
    peers += greet(column < head_count - 1, {"head": column + 1})
    for other in range(ctx_count):
        meets = (me != other) if other % spacing == 0 else (me != other) & owns
        peers += greet(meets, {"ctx": other})
    pl.semaphore_wait(barrier, peers)

    def slot(owner):
        return gathered.at[pl.ds(pl.multiple_of(owner * shard, shard), shard)]

    def passing(owner, up):
        return pltpu.make_async_remote_copy(
            src_ref=slot(owner),
            dst_ref=slot(owner),
            send_sem=(up_send if up else down_send).at[owner],
            recv_sem=gather_recv.at[owner],
            device_id={"head": lax.rem(column + (1 if up else head_count - 1), head_count)},
            device_id_type=MESH,
        )

    gathered[pl.ds(pl.multiple_of(column * shard, shard), shard)] = grad_ref[...]

    def send_on(owner, up):
        @pl.when(column < head_count - 1 if up else column > 0)
        def _():
            passing(owner, up).start()

    send_on(column, True)
    send_on(column, False)

    rates[...] = jnp.zeros_like(rates)
    rates[pl.ds(0, house * heads)] = rate_ref[...]
    rates[...] = jnp.transpose(rates[...])

    lanes = lax.broadcasted_iota(jnp.int32, (tokens, tokens), 1)

    def rate_of(head):
        parts = [
            jnp.sum(jnp.where(lanes == head * house + j, rates[...], 0.0), axis=1, keepdims=True)
            for j in range(house)
        ]
        return jnp.concatenate(parts, axis=0)

    def columns(head):
        return pl.ds(pl.multiple_of(head * HEAD_DIM, HEAD_DIM), HEAD_DIM)

    def load(ref, head):
        return ref[:, :, columns(head)].reshape(rows, HEAD_DIM)

    def to_owner(kept, landing, send, recv, head, source):
        return pltpu.make_async_remote_copy(
            src_ref=kept.at[head], dst_ref=landing.at[source], send_sem=send.at[head],
            recv_sem=recv.at[source], device_id={"ctx": head * spacing}, device_id_type=MESH,
        )

    def give(kept, landing, send, recv, head):
        away = me != head * spacing

        @pl.when(away)
        def _():
            to_owner(kept, landing, send, recv, head, me).start()

        @pl.when(jnp.logical_not(away))
        def _():
            landing[me] = kept[head]

    decay_args = (decay, decay_in, decay_send, decay_recv)
    offset_args = (offset, offset_in, offset_send, offset_recv)
    grad_args = (local_grad, grad_in, grad_send, grad_recv)

    def to_user(made, landing, send, recv, user, head):
        return pltpu.make_async_remote_copy(
            src_ref=made.at[user], dst_ref=landing.at[head], send_sem=send.at[user],
            recv_sem=recv.at[head], device_id={"ctx": user}, device_id_type=MESH,
        )

    def hand_out(made, landing, send, recv, user):
        @pl.when(me != user)
        def _():
            to_user(made, landing, send, recv, user, mine).start()

        @pl.when(me == user)
        def _():
            landing[mine] = made[user]

    state_args = (states, state, state_send, state_recv)
    adjoint_args = (adjoints, adjoint, adjoint_send, adjoint_recv)

    def solve_head(head):
        results = solve_part(
            query_ref[:, columns(head)], load(raw_ref, head), load(value_ref, head), rate_of(head),
            jnp.concatenate([rate_ref[pl.ds(head * house + j, 1)] for j in range(house)], axis=1), house,
        )
        kept = (gram, solver, solved_k, solved_v, decay, offset, scores, reading, scalings)
        for ref, result in zip(kept, results):
            ref[head] = result.astype(ref.dtype)

    together = 2 if heads % 2 == 0 else 1
    turns = heads // together

    def gather_turn(turn):
        for owner, up in ((column - turn, True), (column + turn, False)):
            @pl.when((owner >= 0) & (owner < head_count))
            def _():
                passing(owner, up).wait_recv()
                send_on(owner, up)

    def solve_turn(turn, carry):
        for part in range(together):
            solve_head(turn * together + part)
        for part in range(together):
            give(*decay_args, turn * together + part)
            give(*offset_args, turn * together + part)

        @pl.when((turn + 1) < head_count)
        def _():
            gather_turn(turn + 1)

        return carry

    lax.fori_loop(0, turns, solve_turn, 0)
    for turn in range(turns + 1, head_count):
        gather_turn(turn)

    weight_copy.wait()

    def grad_turn(turn, carry):
        part = pl.ds(pl.multiple_of(turn * together * HEAD_DIM, HEAD_DIM), together * HEAD_DIM)
        block = product(gathered[...], weight[part, :], 1, 1).astype(BF16)
        for index in range(together):
            head = turn * together + index
            grad = block[:, index * HEAD_DIM : (index + 1) * HEAD_DIM]
            grads[head] = grad
            local_grad[head] = product(reading[head], grad, 0, 0)
            give(*grad_args, head)
        return carry

    lax.fori_loop(0, turns, grad_turn, 0)

    @pl.when(owns)
    def _():
        def arrive(args, source):
            @pl.when(me != source)
            def _():
                to_owner(*args, mine, source).wait_recv()

        def forward(user, held):
            states[user] = held
            hand_out(*state_args, user)
            arrive(decay_args, user)
            arrive(offset_args, user)
            return held + offset_in[user] - product(decay_in[user], held, 1, 0)

        zero = jnp.zeros((HEAD_DIM, HEAD_DIM), F32)
        lax.fori_loop(0, ctx_count, forward, zero)

        def backward(step, held):
            user = ctx_count - 1 - step
            adjoints[user] = held
            hand_out(*adjoint_args, user)
            arrive(grad_args, user)
            return held + grad_in[user] - product(decay_in[user], held, 0, 0)

        lax.fori_loop(0, ctx_count, backward, zero)

    def early_head(head):
        @pl.when(me != head * spacing)
        def _():
            to_user(*state_args, me, head).wait_recv()

    def early_turn(turn, carry):
        for part in range(together):
            early_head(turn * together + part)
        for part in range(together):
            head = turn * together + part
            results = early_part(
                query_ref[:, columns(head)], load(raw_ref, head), load(value_ref, head), gram[head],
                solved_k[head], solved_v[head], scores[head], scalings[head, 0:1], grads[head], state[head],
            )
            solved_v[head], errors[head], grad_weighted[head] = results[:3]
            out_query[:, columns(head)] = results[3].astype(BF16)
            grad_key[head] = results[4]
        return carry

    lax.fori_loop(0, turns, early_turn, 0)

    def late_turn(turn, total):
        for part in range(together):
            head = turn * together + part

            @pl.when(me != head * spacing)
            def _():
                to_user(*adjoint_args, me, head).wait_recv()

        for part in range(together):
            head = turn * together + part
            grad_raw, grad_value, grad_rate = late_part(
                load(raw_ref, head), rate_of(head), solver[head], scalings[head, 0:1], solved_v[head],
                errors[head], grad_weighted[head], grad_key[head], state[head], adjoint[head], house,
            )
            out_key[:, :, columns(head)] = grad_raw.reshape(house, tokens, HEAD_DIM).astype(BF16)
            out_value[:, :, columns(head)] = grad_value.reshape(house, tokens, HEAD_DIM).astype(BF16)
            for j in range(house):
                total = jnp.where(
                    lanes == head * house + j, grad_rate[j * tokens : (j + 1) * tokens], total
                )
        return total

    total = lax.fori_loop(0, turns, late_turn, jnp.zeros((tokens, tokens), F32))
    out_rate[...] = jnp.transpose(total)[: house * heads]

    def given(head, carry):
        @pl.when(me != head * spacing)
        def _():
            for args in (decay_args, offset_args, grad_args):
                to_owner(*args, head, me).wait_send()

        return carry

    lax.fori_loop(0, heads, given, 0)

    def handed(user, carry):
        @pl.when(owns & (me != user))
        def _():
            for args in (state_args, adjoint_args):
                to_user(*args, user, mine).wait_send()

        return carry

    lax.fori_loop(0, ctx_count, handed, 0)
    for owner in range(head_count):
        @pl.when((owner <= column) & (column < head_count - 1))
        def _():
            passing(owner, True).wait_send()

        @pl.when((owner >= column) & (column > 0))
        def _():
            passing(owner, False).wait_send()


def hand_over(*refs):
    done = refs[-1]
    copies = [pltpu.make_async_copy(refs[i], refs[4 + i], done.at[i]) for i in range(4)]
    for copy in copies:
        copy.start()
    for copy in copies:
        copy.wait()


def shards(queries, key_input, value_input, beta_rates, out_grad, out_weight):
    house, tokens, width = key_input.shape
    heads = width // HEAD_DIM
    rows = house * tokens
    square = (HEAD_DIM, HEAD_DIM)
    ctx_count, head_count = lax.axis_size("ctx"), lax.axis_size("head")
    vmem = pl.BlockSpec(memory_space=pltpu.VMEM)

    def held(*shape, dtype=F32):
        return pltpu.VMEM((heads,) + shape, dtype)

    results = pl.pallas_call(
        functools.partial(kernel, ctx_count, head_count),
        out_shape=(
            jax.ShapeDtypeStruct(queries.shape, BF16),
            jax.ShapeDtypeStruct(key_input.shape, BF16),
            jax.ShapeDtypeStruct(value_input.shape, BF16),
            jax.ShapeDtypeStruct((heads * house, tokens), F32),
        ),
        in_specs=[vmem] * 5 + [pl.BlockSpec(memory_space=pl.ANY)],
        out_specs=(vmem,) * 4,
        scratch_shapes=[
            pltpu.VMEM(out_weight.shape, BF16),
            pltpu.VMEM((tokens, out_grad.shape[1]), BF16),
            pltpu.VMEM((tokens, tokens), F32),
            held(tokens, HEAD_DIM, dtype=BF16),
            held(rows, rows, dtype=BF16),
            held(rows, rows, dtype=SOLVER),
            held(rows, HEAD_DIM),
            held(rows, HEAD_DIM),
            held(*square, dtype=BF16),
            held(*square),
            held(tokens, rows, dtype=BF16),
            held(tokens, HEAD_DIM, dtype=BF16),
            held(*square),
            held(8, rows),
            held(rows, HEAD_DIM),
            held(rows, HEAD_DIM),
            held(rows, HEAD_DIM),
            held(*square),
            held(*square),
            pltpu.VMEM((ctx_count,) + square, BF16),
            pltpu.VMEM((ctx_count,) + square, F32),
            pltpu.VMEM((ctx_count,) + square, F32),
            pltpu.VMEM((ctx_count,) + square, F32),
            pltpu.VMEM((ctx_count,) + square, F32),
            pltpu.SemaphoreType.DMA,
        ]
        + [
            pltpu.SemaphoreType.DMA((count,))
            for count in (head_count,) * 3 + (heads, ctx_count) * 3 + (ctx_count, heads) * 2
        ],
        compiler_params=pltpu.CompilerParams(
            collective_id=0, has_side_effects=True, vmem_limit_bytes=56 * 1024 * 1024
        ),
    )(
        queries,
        key_input,
        value_input,
        beta_rates.reshape(heads * house, tokens),
        out_grad,
        out_weight,
    )
    results = pl.pallas_call(
        hand_over,
        out_shape=[jax.ShapeDtypeStruct(result.shape, result.dtype) for result in results],
        in_specs=[pl.BlockSpec(memory_space=pl.ANY)] * 4,
        out_specs=[pl.BlockSpec(memory_space=pl.ANY)] * 4,
        scratch_shapes=[pltpu.SemaphoreType.DMA((4,))],
    )(*results)
    return tuple(results[:3]) + (results[3].reshape(beta_rates.shape),)


def solution(mesh):
    placed = (
        P("ctx", "head"),
        P(None, "ctx", "head"),
        P(None, "ctx", "head"),
        P("head", None, "ctx"),
        P(("ctx", "head"), None),
        P("head", None),
    )
    return jax.shard_map(
        shards,
        mesh=mesh,
        in_specs=placed,
        out_specs=placed[:4],
        check_vma=False,
    )
```

```python
import functools

import jax
import jax.numpy as jnp
from jax import lax
from jax.experimental import pallas as pl
from jax.experimental.pallas import tpu as pltpu
from jax.sharding import PartitionSpec as P

HEAD_DIM = 128
MESH = pl.DeviceIdType.MESH
F32 = jnp.float32
BF16 = jnp.bfloat16
SOLVER = BF16
SPLIT = {
    "inv": "lr", "sk": "l", "sv": "l", "maps": "r", "rd": "lr", "w": "", "gs": "", "q1": "",
    "q2": "", "k1": "", "gw2": "", "un": "r", "gg": "", "k2": "", "k4": "l",
}


def product(left, right, over_left, over_right, split=""):
    def one(a, b):
        return lax.dot_general(
            a, b, (((over_left,), (over_right,)), ((), ())), preferred_element_type=F32
        )

    left_high, right_high = left.astype(BF16), right.astype(BF16)
    total = one(left_high, right_high)
    if "l" in split and left.dtype == F32:
        total += one((left - left_high.astype(F32)).astype(BF16), right_high)
    if "r" in split and right.dtype == F32:
        total += one(left_high, (right - right_high.astype(F32)).astype(BF16))
    return total


def order(shape, axis, tokens, house):
    index = lax.broadcasted_iota(jnp.int32, shape, axis)
    return house * (index % tokens) + index // tokens


def inverse(strict_system, tokens, house):
    shape = strict_system.shape
    rows = shape[0]
    apart = order(shape, 0, tokens, house) ^ order(shape, 1, tokens, house)
    result = -jnp.where(apart == 1, strict_system, 0.0)
    size = 2
    while size < rows:
        corner = jnp.where((apart >= size) & (apart < 2 * size), strict_system, 0.0)
        span = size // house
        split = SPLIT["inv"] if 4 * size >= rows else ""
        if span % 8:
            half = corner + product(corner, result, 1, 0, split)
            result = result - half - product(result, half, 1, 0, split)
        else:
            pairs = (house, tokens // (2 * span), 2, span, rows)

            def second(array):
                return array.reshape(pairs)[:, :, 1].reshape(rows // 2, rows)

            def joined(first, last):
                parts = [part.reshape(pairs[:2] + (1, span, rows)) for part in (first, last)]
                return jnp.concatenate(parts, axis=2).reshape(shape)

            half = second(corner)
            half = half + product(half, result, 1, 0, split)
            lower = second(result)
            whole = joined(jnp.zeros_like(half), half)
            lower = lower - half - product(lower, whole, 1, 0, split)
            result = joined(result.reshape(pairs)[:, :, 0].reshape(rows // 2, rows), lower)
        size *= 2
    return result


def scaling_of(raw):
    raw = raw.astype(F32)
    return lax.rsqrt(jnp.sum(raw * raw, axis=-1, keepdims=True) + 1e-06)


def read_mask(tokens, rows):
    reader = lax.broadcasted_iota(jnp.int32, (tokens, rows), 0)
    return lax.broadcasted_iota(jnp.int32, (tokens, rows), 1) % tokens <= reader


def strict_mask(tokens, house):
    shape = (house * tokens, house * tokens)
    return order(shape, 1, tokens, house) < order(shape, 0, tokens, house)


def solve_part(query, raw, value, rate, rate_row, house):
    tokens = query.shape[0]
    rows = raw.shape[0]
    scaling = scaling_of(raw)
    index = [lax.broadcasted_iota(jnp.int32, (rows, rows), axis) for axis in (0, 1)]
    scaling_row = jnp.sum(jnp.where(index[0] == index[1], scaling, 0.0), axis=0, keepdims=True)
    gram = product(raw, raw, 1, 1)
    gram = jnp.where(strict_mask(tokens, house), gram * scaling * scaling_row, 0.0)
    solver = inverse(gram * rate, tokens, house)
    scaled_raw = raw.astype(F32) * (scaling * rate)
    solved_k = scaled_raw + product(solver * (rate_row * scaling_row), raw, 1, 0, SPLIT["sk"])
    solved_v = value.astype(F32) * rate + product(solver * rate_row, value, 1, 0, SPLIT["sv"])
    both = jnp.concatenate([solved_k * scaling, solved_v * scaling], axis=1)
    maps = product(raw, both, 0, 0, SPLIT["maps"])
    scores = product(query, raw, 1, 1) * (scaling_row * HEAD_DIM ** (-0.5))
    scores = jnp.where(read_mask(tokens, rows), scores, 0.0)
    reading = query.astype(F32) * HEAD_DIM ** (-0.5) - product(scores, solved_k, 1, 0, SPLIT["rd"])
    return (
        gram, solver, solved_k, solved_v, maps[:, :HEAD_DIM], maps[:, HEAD_DIM:], scores, reading,
        jnp.broadcast_to(scaling_row, (8, rows)),
    )


def early_part(query, raw, value, gram, solved_k, solved_v, scores, scaling_row, grad, state):
    tokens = query.shape[0]
    weighted = product(solved_k, state, 1, 0, SPLIT["w"]) - solved_v
    errors = product(raw, state, 1, 0) * scaling_of(raw) - value.astype(F32)
    errors = errors - product(gram, weighted, 1, 0)
    grad_weighted = -product(scores, grad, 0, 0)
    grad_scores = -product(grad, weighted, 1, 1, SPLIT["gs"]) * HEAD_DIM ** (-0.5)
    grad_scores = jnp.where(read_mask(tokens, raw.shape[0]), grad_scores, 0.0)
    grad_query = product(grad, state, 1, 1, SPLIT["q1"]) * HEAD_DIM ** (-0.5)
    grad_query = grad_query + product(grad_scores * scaling_row, raw, 1, 0, SPLIT["q2"])
    grad_key = product(grad_scores, query, 0, 0, SPLIT["k1"])
    return weighted, errors, grad_weighted, grad_query, grad_key


def late_part(
    raw, rate, solver, scaling_row, weighted, errors, grad_weighted, grad_key, state, adjoint, house
):
    tokens = raw.shape[0] // house
    scaling = scaling_of(raw)
    key = raw.astype(F32) * scaling
    grad_weighted = grad_weighted - product(raw, adjoint, 1, 0, SPLIT["gw2"]) * scaling
    unscaled = grad_weighted + product(solver, grad_weighted, 0, 0, SPLIT["un"])
    pulled = unscaled * rate
    grad_rate = jnp.sum(errors * unscaled, axis=1, keepdims=True)
    grad_gram = jnp.where(strict_mask(tokens, house), product(pulled, weighted, 1, 1, SPLIT["gg"]), 0.0)
    grad_gram = (grad_gram + jnp.transpose(grad_gram)) * scaling_row
    rows_side = jnp.concatenate([-weighted, pulled], axis=1)
    state_side = jnp.concatenate([adjoint, state], axis=1)
    grad_key = grad_key + product(rows_side, state_side, 1, 1, SPLIT["k2"])
    grad_key = grad_key - product(grad_gram, raw, 1, 0, SPLIT["k4"])
    along = jnp.sum(grad_key * key, axis=1, keepdims=True)
    grad_raw = scaling * (grad_key - key * along)
    return grad_raw, -pulled, grad_rate


def kernel(
    ctx_count,
    head_count,
    query_ref, raw_ref, value_ref, rate_ref, grad_ref, weight_ref,
    out_query, out_key, out_value, out_rate,
    weight, gathered, rates, grads,
    gram, solver, solved_k, solved_v, decay, offset, scores, reading, local_grad,
    scalings, errors, grad_weighted, grad_key, state, adjoint,
    decay_in, offset_in, grad_in, states, adjoints,
    weight_sem, up_send, down_send, gather_recv,
    decay_send, decay_recv, offset_send, offset_recv, grad_send, grad_recv,
    state_send, state_recv, adjoint_send, adjoint_recv,
):
    me, column = lax.axis_index("ctx"), lax.axis_index("head")
    house, tokens = raw_ref.shape[0], raw_ref.shape[1]
    heads = state.shape[0]
    shard = grad_ref.shape[0]
    rows = house * tokens
    spacing = ctx_count // heads
    owns = lax.rem(me, spacing) == 0
    mine = me // spacing

    weight_copy = pltpu.make_async_copy(weight_ref, weight, weight_sem)
    weight_copy.start()

    barrier = pltpu.get_barrier_semaphore()

    def greet(there, device):
        @pl.when(there)
        def _():
            pl.semaphore_signal(barrier, inc=1, device_id=device, device_id_type=MESH)

        return there.astype(jnp.int32)

    peers = greet(column > 0, {"head": column - 1})
    peers += greet(column < head_count - 1, {"head": column + 1})
    for other in range(ctx_count):
        meets = (me != other) if other % spacing == 0 else (me != other) & owns
        peers += greet(meets, {"ctx": other})
    pl.semaphore_wait(barrier, peers)

    def slot(owner):
        return gathered.at[pl.ds(pl.multiple_of(owner * shard, shard), shard)]

    def passing(owner, up):
        return pltpu.make_async_remote_copy(
            src_ref=slot(owner),
            dst_ref=slot(owner),
            send_sem=(up_send if up else down_send).at[owner],
            recv_sem=gather_recv.at[owner],
            device_id={"head": lax.rem(column + (1 if up else head_count - 1), head_count)},
            device_id_type=MESH,
        )

    gathered[pl.ds(pl.multiple_of(column * shard, shard), shard)] = grad_ref[...]

    def send_on(owner, up):
        @pl.when(column < head_count - 1 if up else column > 0)
        def _():
            passing(owner, up).start()

    send_on(column, True)
    send_on(column, False)

    rates[...] = jnp.zeros_like(rates)
    rates[pl.ds(0, house * heads)] = rate_ref[...]
    rates[...] = jnp.transpose(rates[...])

    lanes = lax.broadcasted_iota(jnp.int32, (tokens, tokens), 1)

    def rate_of(head):
        parts = [
            jnp.sum(jnp.where(lanes == head * house + j, rates[...], 0.0), axis=1, keepdims=True)
            for j in range(house)
        ]
        return jnp.concatenate(parts, axis=0)

    def columns(head):
        return pl.ds(pl.multiple_of(head * HEAD_DIM, HEAD_DIM), HEAD_DIM)

    def load(ref, head):
        return ref[:, :, columns(head)].reshape(rows, HEAD_DIM)

    def to_owner(kept, landing, send, recv, head, source):
        return pltpu.make_async_remote_copy(
            src_ref=kept.at[head], dst_ref=landing.at[source], send_sem=send.at[head],
            recv_sem=recv.at[source], device_id={"ctx": head * spacing}, device_id_type=MESH,
        )

    def give(kept, landing, send, recv, head):
        away = me != head * spacing

        @pl.when(away)
        def _():
            to_owner(kept, landing, send, recv, head, me).start()

        @pl.when(jnp.logical_not(away))
        def _():
            landing[me] = kept[head]

    decay_args = (decay, decay_in, decay_send, decay_recv)
    offset_args = (offset, offset_in, offset_send, offset_recv)
    grad_args = (local_grad, grad_in, grad_send, grad_recv)

    def to_user(made, landing, send, recv, user, head):
        return pltpu.make_async_remote_copy(
            src_ref=made.at[user], dst_ref=landing.at[head], send_sem=send.at[user],
            recv_sem=recv.at[head], device_id={"ctx": user}, device_id_type=MESH,
        )

    def hand_out(made, landing, send, recv, user):
        @pl.when(me != user)
        def _():
            to_user(made, landing, send, recv, user, mine).start()

        @pl.when(me == user)
        def _():
            landing[mine] = made[user]

    state_args = (states, state, state_send, state_recv)
    adjoint_args = (adjoints, adjoint, adjoint_send, adjoint_recv)

    def solve_head(head):
        results = solve_part(
            query_ref[:, columns(head)], load(raw_ref, head), load(value_ref, head), rate_of(head),
            jnp.concatenate([rate_ref[pl.ds(head * house + j, 1)] for j in range(house)], axis=1), house,
        )
        kept = (gram, solver, solved_k, solved_v, decay, offset, scores, reading, scalings)
        for ref, result in zip(kept, results):
            ref[head] = result.astype(ref.dtype)

    together = 2 if heads % 2 == 0 else 1
    turns = heads // together

    def gather_turn(turn):
        for owner, up in ((column - turn, True), (column + turn, False)):
            @pl.when((owner >= 0) & (owner < head_count))
            def _():
                passing(owner, up).wait_recv()
                send_on(owner, up)

    def solve_turn(turn, carry):
        for part in range(together):
            solve_head(turn * together + part)
        for part in range(together):
            give(*decay_args, turn * together + part)
            give(*offset_args, turn * together + part)

        @pl.when((turn + 1) < head_count)
        def _():
            gather_turn(turn + 1)

        return carry

    lax.fori_loop(0, turns, solve_turn, 0)
    for turn in range(turns + 1, head_count):
        gather_turn(turn)

    weight_copy.wait()

    def grad_turn(turn, carry):
        part = pl.ds(pl.multiple_of(turn * together * HEAD_DIM, HEAD_DIM), together * HEAD_DIM)
        block = product(gathered[...], weight[part, :], 1, 1).astype(BF16)
        for index in range(together):
            head = turn * together + index
            grad = block[:, index * HEAD_DIM : (index + 1) * HEAD_DIM]
            grads[head] = grad
            local_grad[head] = product(reading[head], grad, 0, 0)
            give(*grad_args, head)
        return carry

    lax.fori_loop(0, turns, grad_turn, 0)

    @pl.when(owns)
    def _():
        def arrive(args, source):
            @pl.when(me != source)
            def _():
                to_owner(*args, mine, source).wait_recv()

        def forward(user, held):
            states[user] = held
            hand_out(*state_args, user)
            arrive(decay_args, user)
            arrive(offset_args, user)
            return held + offset_in[user] - product(decay_in[user], held, 1, 0)

        zero = jnp.zeros((HEAD_DIM, HEAD_DIM), F32)
        lax.fori_loop(0, ctx_count, forward, zero)

        def backward(step, held):
            user = ctx_count - 1 - step
            adjoints[user] = held
            hand_out(*adjoint_args, user)
            arrive(grad_args, user)
            return held + grad_in[user] - product(decay_in[user], held, 0, 0)

        lax.fori_loop(0, ctx_count, backward, zero)

    def early_head(head):
        @pl.when(me != head * spacing)
        def _():
            to_user(*state_args, me, head).wait_recv()

    def early_turn(turn, carry):
        for part in range(together):
            early_head(turn * together + part)
        for part in range(together):
            head = turn * together + part
            results = early_part(
                query_ref[:, columns(head)], load(raw_ref, head), load(value_ref, head), gram[head],
                solved_k[head], solved_v[head], scores[head], scalings[head, 0:1], grads[head], state[head],
            )
            solved_v[head], errors[head], grad_weighted[head] = results[:3]
            out_query[:, columns(head)] = results[3].astype(BF16)
            grad_key[head] = results[4]
        return carry

    lax.fori_loop(0, turns, early_turn, 0)

    def late_turn(turn, total):
        for part in range(together):
            head = turn * together + part

            @pl.when(me != head * spacing)
            def _():
                to_user(*adjoint_args, me, head).wait_recv()

        for part in range(together):
            head = turn * together + part
            grad_raw, grad_value, grad_rate = late_part(
                load(raw_ref, head), rate_of(head), solver[head], scalings[head, 0:1], solved_v[head],
                errors[head], grad_weighted[head], grad_key[head], state[head], adjoint[head], house,
            )
            out_key[:, :, columns(head)] = grad_raw.reshape(house, tokens, HEAD_DIM).astype(BF16)
            out_value[:, :, columns(head)] = grad_value.reshape(house, tokens, HEAD_DIM).astype(BF16)
            for j in range(house):
                total = jnp.where(
                    lanes == head * house + j, grad_rate[j * tokens : (j + 1) * tokens], total
                )
        return total

    total = lax.fori_loop(0, turns, late_turn, jnp.zeros((tokens, tokens), F32))
    out_rate[...] = jnp.transpose(total)[: house * heads]

    def given(head, carry):
        @pl.when(me != head * spacing)
        def _():
            for args in (decay_args, offset_args, grad_args):
                to_owner(*args, head, me).wait_send()

        return carry

    lax.fori_loop(0, heads, given, 0)

    def handed(user, carry):
        @pl.when(owns & (me != user))
        def _():
            for args in (state_args, adjoint_args):
                to_user(*args, user, mine).wait_send()

        return carry

    lax.fori_loop(0, ctx_count, handed, 0)
    for owner in range(head_count):
        @pl.when((owner <= column) & (column < head_count - 1))
        def _():
            passing(owner, True).wait_send()

        @pl.when((owner >= column) & (column > 0))
        def _():
            passing(owner, False).wait_send()


def hand_over(*refs):
    for source, target in zip(refs[:4], refs[4:]):
        target[...] = source[...]


def shards(queries, key_input, value_input, beta_rates, out_grad, out_weight):
    house, tokens, width = key_input.shape
    heads = width // HEAD_DIM
    rows = house * tokens
    square = (HEAD_DIM, HEAD_DIM)
    ctx_count, head_count = lax.axis_size("ctx"), lax.axis_size("head")
    vmem = pl.BlockSpec(memory_space=pltpu.VMEM)

    def held(*shape, dtype=F32):
        return pltpu.VMEM((heads,) + shape, dtype)

    results = pl.pallas_call(
        functools.partial(kernel, ctx_count, head_count),
        out_shape=(
            jax.ShapeDtypeStruct(queries.shape, BF16),
            jax.ShapeDtypeStruct(key_input.shape, BF16),
            jax.ShapeDtypeStruct(value_input.shape, BF16),
            jax.ShapeDtypeStruct((heads * house, tokens), F32),
        ),
        in_specs=[vmem] * 5 + [pl.BlockSpec(memory_space=pl.ANY)],
        out_specs=(vmem,) * 4,
        scratch_shapes=[
            pltpu.VMEM(out_weight.shape, BF16),
            pltpu.VMEM((tokens, out_grad.shape[1]), BF16),
            pltpu.VMEM((tokens, tokens), F32),
            held(tokens, HEAD_DIM, dtype=BF16),
            held(rows, rows, dtype=BF16),
            held(rows, rows, dtype=SOLVER),
            held(rows, HEAD_DIM),
            held(rows, HEAD_DIM),
            held(*square, dtype=BF16),
            held(*square),
            held(tokens, rows, dtype=BF16),
            held(tokens, HEAD_DIM, dtype=BF16),
            held(*square),
            held(8, rows),
            held(rows, HEAD_DIM),
            held(rows, HEAD_DIM),
            held(rows, HEAD_DIM),
            held(*square),
            held(*square),
            pltpu.VMEM((ctx_count,) + square, BF16),
            pltpu.VMEM((ctx_count,) + square, F32),
            pltpu.VMEM((ctx_count,) + square, F32),
            pltpu.VMEM((ctx_count,) + square, F32),
            pltpu.VMEM((ctx_count,) + square, F32),
            pltpu.SemaphoreType.DMA,
        ]
        + [
            pltpu.SemaphoreType.DMA((count,))
            for count in (head_count,) * 3 + (heads, ctx_count) * 3 + (ctx_count, heads) * 2
        ],
        compiler_params=pltpu.CompilerParams(
            collective_id=0, has_side_effects=True, vmem_limit_bytes=56 * 1024 * 1024
        ),
    )(
        queries,
        key_input,
        value_input,
        beta_rates.reshape(heads * house, tokens),
        out_grad,
        out_weight,
    )
    results = pl.pallas_call(
        hand_over,
        out_shape=[jax.ShapeDtypeStruct(result.shape, result.dtype) for result in results],
        in_specs=[vmem] * 4,
        out_specs=[vmem] * 4,
    )(*results)
    return tuple(results[:3]) + (results[3].reshape(beta_rates.shape),)


def solution(mesh):
    placed = (
        P("ctx", "head"),
        P(None, "ctx", "head"),
        P(None, "ctx", "head"),
        P("head", None, "ctx"),
        P(("ctx", "head"), None),
        P("head", None),
    )
    return jax.shard_map(
        shards,
        mesh=mesh,
        in_specs=placed,
        out_specs=placed[:4],
        check_vma=False,
    )
```

```python
import functools

import jax
import jax.numpy as jnp
from jax import lax
from jax.experimental import pallas as pl
from jax.experimental.pallas import tpu as pltpu
from jax.sharding import PartitionSpec as P

HEAD_DIM = 128
MESH = pl.DeviceIdType.MESH
F32 = jnp.float32
BF16 = jnp.bfloat16
SOLVER = BF16
SPLIT = {
    "inv": "lr", "sk": "l", "sv": "l", "maps": "r", "rd": "lr", "w": "", "gs": "", "q1": "",
    "q2": "", "k1": "", "gw2": "", "un": "r", "gg": "", "k2": "", "k4": "l",
}


def product(left, right, over_left, over_right, split=""):
    def one(a, b):
        return lax.dot_general(
            a, b, (((over_left,), (over_right,)), ((), ())), preferred_element_type=F32
        )

    left_high, right_high = left.astype(BF16), right.astype(BF16)
    total = one(left_high, right_high)
    if "l" in split and left.dtype == F32:
        total += one((left - left_high.astype(F32)).astype(BF16), right_high)
    if "r" in split and right.dtype == F32:
        total += one(left_high, (right - right_high.astype(F32)).astype(BF16))
    return total


def order(shape, axis, tokens, house):
    index = lax.broadcasted_iota(jnp.int32, shape, axis)
    return house * (index % tokens) + index // tokens


def inverse(strict_system, tokens, house):
    shape = strict_system.shape
    rows = shape[0]
    apart = order(shape, 0, tokens, house) ^ order(shape, 1, tokens, house)
    result = -jnp.where(apart == 1, strict_system, 0.0)
    size = 2
    while size < rows:
        corner = jnp.where((apart >= size) & (apart < 2 * size), strict_system, 0.0)
        span = size // house
        split = SPLIT["inv"] if 4 * size >= rows else ""
        if span % 8:
            half = corner + product(corner, result, 1, 0, split)
            result = result - half - product(result, half, 1, 0, split)
        else:
            pairs = (house, tokens // (2 * span), 2, span, rows)

            def second(array):
                return array.reshape(pairs)[:, :, 1].reshape(rows // 2, rows)

            def joined(first, last):
                parts = [part.reshape(pairs[:2] + (1, span, rows)) for part in (first, last)]
                return jnp.concatenate(parts, axis=2).reshape(shape)

            half = second(corner)
            half = half + product(half, result, 1, 0, split)
            lower = second(result)
            whole = joined(jnp.zeros_like(half), half)
            lower = lower - half - product(lower, whole, 1, 0, split)
            result = joined(result.reshape(pairs)[:, :, 0].reshape(rows // 2, rows), lower)
        size *= 2
    return result


def scaling_of(raw):
    raw = raw.astype(F32)
    return lax.rsqrt(jnp.sum(raw * raw, axis=-1, keepdims=True) + 1e-06)


def read_mask(tokens, rows):
    reader = lax.broadcasted_iota(jnp.int32, (tokens, rows), 0)
    return lax.broadcasted_iota(jnp.int32, (tokens, rows), 1) % tokens <= reader


def strict_mask(tokens, house):
    shape = (house * tokens, house * tokens)
    return order(shape, 1, tokens, house) < order(shape, 0, tokens, house)


def solve_part(query, raw, value, rate, rate_row, house):
    tokens = query.shape[0]
    rows = raw.shape[0]
    scaling = scaling_of(raw)
    index = [lax.broadcasted_iota(jnp.int32, (rows, rows), axis) for axis in (0, 1)]
    scaling_row = jnp.sum(jnp.where(index[0] == index[1], scaling, 0.0), axis=0, keepdims=True)
    gram = product(raw, raw, 1, 1)
    gram = jnp.where(strict_mask(tokens, house), gram * scaling * scaling_row, 0.0)
    solver = inverse(gram * rate, tokens, house)
    scaled_raw = raw.astype(F32) * (scaling * rate)
    solved_k = scaled_raw + product(solver * (rate_row * scaling_row), raw, 1, 0, SPLIT["sk"])
    solved_v = value.astype(F32) * rate + product(solver * rate_row, value, 1, 0, SPLIT["sv"])
    both = jnp.concatenate([solved_k * scaling, solved_v * scaling], axis=1)
    maps = product(raw, both, 0, 0, SPLIT["maps"])
    scores = product(query, raw, 1, 1) * (scaling_row * HEAD_DIM ** (-0.5))
    scores = jnp.where(read_mask(tokens, rows), scores, 0.0)
    reading = query.astype(F32) * HEAD_DIM ** (-0.5) - product(scores, solved_k, 1, 0, SPLIT["rd"])
    return (
        gram, solver, solved_k, solved_v, maps[:, :HEAD_DIM], maps[:, HEAD_DIM:], scores, reading,
        jnp.broadcast_to(scaling_row, (8, rows)),
    )


def early_part(query, raw, value, gram, solved_k, solved_v, scores, scaling_row, grad, state):
    tokens = query.shape[0]
    weighted = product(solved_k, state, 1, 0, SPLIT["w"]) - solved_v
    errors = product(raw, state, 1, 0) * scaling_of(raw) - value.astype(F32)
    errors = errors - product(gram, weighted, 1, 0)
    grad_weighted = -product(scores, grad, 0, 0)
    grad_scores = -product(grad, weighted, 1, 1, SPLIT["gs"]) * HEAD_DIM ** (-0.5)
    grad_scores = jnp.where(read_mask(tokens, raw.shape[0]), grad_scores, 0.0)
    grad_query = product(grad, state, 1, 1, SPLIT["q1"]) * HEAD_DIM ** (-0.5)
    grad_query = grad_query + product(grad_scores * scaling_row, raw, 1, 0, SPLIT["q2"])
    grad_key = product(grad_scores, query, 0, 0, SPLIT["k1"])
    return weighted, errors, grad_weighted, grad_query, grad_key


def late_part(
    raw, rate, solver, scaling_row, weighted, errors, grad_weighted, grad_key, state, adjoint, house
):
    tokens = raw.shape[0] // house
    scaling = scaling_of(raw)
    key = raw.astype(F32) * scaling
    grad_weighted = grad_weighted - product(raw, adjoint, 1, 0, SPLIT["gw2"]) * scaling
    unscaled = grad_weighted + product(solver, grad_weighted, 0, 0, SPLIT["un"])
    pulled = unscaled * rate
    grad_rate = jnp.sum(errors * unscaled, axis=1, keepdims=True)
    grad_gram = jnp.where(strict_mask(tokens, house), product(pulled, weighted, 1, 1, SPLIT["gg"]), 0.0)
    grad_gram = (grad_gram + jnp.transpose(grad_gram)) * scaling_row
    rows_side = jnp.concatenate([-weighted, pulled], axis=1)
    state_side = jnp.concatenate([adjoint, state], axis=1)
    grad_key = grad_key + product(rows_side, state_side, 1, 1, SPLIT["k2"])
    grad_key = grad_key - product(grad_gram, raw, 1, 0, SPLIT["k4"])
    along = jnp.sum(grad_key * key, axis=1, keepdims=True)
    grad_raw = scaling * (grad_key - key * along)
    return grad_raw, -pulled, grad_rate


def kernel(
    ctx_count,
    head_count,
    query_ref, raw_ref, value_ref, rate_ref, grad_ref, weight_ref,
    out_query, out_key, out_value, out_rate,
    weight, gathered, rates, grads,
    gram, solver, solved_k, solved_v, decay, offset, scores, reading, local_grad,
    scalings, errors, grad_weighted, grad_key, state, adjoint,
    decay_in, offset_in, grad_in, states, adjoints,
    weight_sem, up_send, down_send, gather_recv,
    decay_send, decay_recv, offset_send, offset_recv, grad_send, grad_recv,
    state_send, state_recv, adjoint_send, adjoint_recv,
):
    me, column = lax.axis_index("ctx"), lax.axis_index("head")
    house, tokens = raw_ref.shape[0], raw_ref.shape[1]
    heads = state.shape[0]
    shard = grad_ref.shape[0]
    rows = house * tokens
    spacing = ctx_count // heads
    owns = lax.rem(me, spacing) == 0
    mine = me // spacing

    weight_copy = pltpu.make_async_copy(weight_ref, weight, weight_sem)
    weight_copy.start()

    barrier = pltpu.get_barrier_semaphore()

    def greet(there, device):
        @pl.when(there)
        def _():
            pl.semaphore_signal(barrier, inc=1, device_id=device, device_id_type=MESH)

        return there.astype(jnp.int32)

    peers = greet(column > 0, {"head": column - 1})
    peers += greet(column < head_count - 1, {"head": column + 1})
    for other in range(ctx_count):
        meets = (me != other) if other % spacing == 0 else (me != other) & owns
        peers += greet(meets, {"ctx": other})
    pl.semaphore_wait(barrier, peers)

    def slot(owner):
        return gathered.at[pl.ds(pl.multiple_of(owner * shard, shard), shard)]

    def passing(owner, up):
        return pltpu.make_async_remote_copy(
            src_ref=slot(owner),
            dst_ref=slot(owner),
            send_sem=(up_send if up else down_send).at[owner],
            recv_sem=gather_recv.at[owner],
            device_id={"head": lax.rem(column + (1 if up else head_count - 1), head_count)},
            device_id_type=MESH,
        )

    gathered[pl.ds(pl.multiple_of(column * shard, shard), shard)] = grad_ref[...]

    def send_on(owner, up):
        @pl.when(column < head_count - 1 if up else column > 0)
        def _():
            passing(owner, up).start()

    send_on(column, True)
    send_on(column, False)

    rates[...] = jnp.zeros_like(rates)
    rates[pl.ds(0, house * heads)] = rate_ref[...]
    rates[...] = jnp.transpose(rates[...])

    lanes = lax.broadcasted_iota(jnp.int32, (tokens, tokens), 1)

    def rate_of(head):
        parts = [
            jnp.sum(jnp.where(lanes == head * house + j, rates[...], 0.0), axis=1, keepdims=True)
            for j in range(house)
        ]
        return jnp.concatenate(parts, axis=0)

    def columns(head):
        return pl.ds(pl.multiple_of(head * HEAD_DIM, HEAD_DIM), HEAD_DIM)

    def load(ref, head):
        return ref[:, :, columns(head)].reshape(rows, HEAD_DIM)

    def to_owner(kept, landing, send, recv, head, source):
        return pltpu.make_async_remote_copy(
            src_ref=kept.at[head], dst_ref=landing.at[source], send_sem=send.at[head],
            recv_sem=recv.at[source], device_id={"ctx": head * spacing}, device_id_type=MESH,
        )

    def give(kept, landing, send, recv, head):
        away = me != head * spacing

        @pl.when(away)
        def _():
            to_owner(kept, landing, send, recv, head, me).start()

        @pl.when(jnp.logical_not(away))
        def _():
            landing[me] = kept[head]

    decay_args = (decay, decay_in, decay_send, decay_recv)
    offset_args = (offset, offset_in, offset_send, offset_recv)
    grad_args = (local_grad, grad_in, grad_send, grad_recv)

    def to_user(made, landing, send, recv, user, head):
        return pltpu.make_async_remote_copy(
            src_ref=made.at[user], dst_ref=landing.at[head], send_sem=send.at[user],
            recv_sem=recv.at[head], device_id={"ctx": user}, device_id_type=MESH,
        )

    def hand_out(made, landing, send, recv, user):
        @pl.when(me != user)
        def _():
            to_user(made, landing, send, recv, user, mine).start()

        @pl.when(me == user)
        def _():
            landing[mine] = made[user]

    state_args = (states, state, state_send, state_recv)
    adjoint_args = (adjoints, adjoint, adjoint_send, adjoint_recv)

    def solve_head(head):
        results = solve_part(
            query_ref[:, columns(head)], load(raw_ref, head), load(value_ref, head), rate_of(head),
            jnp.concatenate([rate_ref[pl.ds(head * house + j, 1)] for j in range(house)], axis=1), house,
        )
        kept = (gram, solver, solved_k, solved_v, decay, offset, scores, reading, scalings)
        for ref, result in zip(kept, results):
            ref[head] = result.astype(ref.dtype)

    together = 2 if heads % 2 == 0 else 1
    turns = heads // together

    def gather_turn(turn):
        for owner, up in ((column - turn, True), (column + turn, False)):
            @pl.when((owner >= 0) & (owner < head_count))
            def _():
                passing(owner, up).wait_recv()
                send_on(owner, up)

    def solve_turn(turn, carry):
        for part in range(together):
            solve_head(turn * together + part)
        for part in range(together):
            give(*decay_args, turn * together + part)
            give(*offset_args, turn * together + part)

        @pl.when((turn + 1) < head_count)
        def _():
            gather_turn(turn + 1)

        return carry

    lax.fori_loop(0, turns, solve_turn, 0)
    for turn in range(turns + 1, head_count):
        gather_turn(turn)

    weight_copy.wait()

    def grad_turn(turn, carry):
        part = pl.ds(pl.multiple_of(turn * together * HEAD_DIM, HEAD_DIM), together * HEAD_DIM)
        block = product(gathered[...], weight[part, :], 1, 1).astype(BF16)
        for index in range(together):
            head = turn * together + index
            grad = block[:, index * HEAD_DIM : (index + 1) * HEAD_DIM]
            grads[head] = grad
            local_grad[head] = product(reading[head], grad, 0, 0).astype(BF16)
            give(*grad_args, head)
        return carry

    lax.fori_loop(0, turns, grad_turn, 0)

    @pl.when(owns)
    def _():
        def arrive(args, source):
            @pl.when(me != source)
            def _():
                to_owner(*args, mine, source).wait_recv()

        def forward(user, held):
            states[user] = held.astype(BF16)
            hand_out(*state_args, user)
            arrive(decay_args, user)
            arrive(offset_args, user)
            return held + offset_in[user] - product(decay_in[user], held, 1, 0)

        zero = jnp.zeros((HEAD_DIM, HEAD_DIM), F32)
        lax.fori_loop(0, ctx_count, forward, zero)

        def backward(step, held):
            user = ctx_count - 1 - step
            adjoints[user] = held.astype(BF16)
            hand_out(*adjoint_args, user)
            arrive(grad_args, user)
            return held + grad_in[user] - product(decay_in[user], held, 0, 0)

        lax.fori_loop(0, ctx_count, backward, zero)

    def early_head(head):
        @pl.when(me != head * spacing)
        def _():
            to_user(*state_args, me, head).wait_recv()

    def early_turn(turn, carry):
        for part in range(together):
            early_head(turn * together + part)
        for part in range(together):
            head = turn * together + part
            results = early_part(
                query_ref[:, columns(head)], load(raw_ref, head), load(value_ref, head), gram[head],
                solved_k[head], solved_v[head], scores[head], scalings[head, 0:1], grads[head], state[head],
            )
            solved_v[head], errors[head], grad_weighted[head] = results[:3]
            out_query[:, columns(head)] = results[3].astype(BF16)
            grad_key[head] = results[4]
        return carry

    lax.fori_loop(0, turns, early_turn, 0)

    def late_turn(turn, total):
        for part in range(together):
            head = turn * together + part

            @pl.when(me != head * spacing)
            def _():
                to_user(*adjoint_args, me, head).wait_recv()

        for part in range(together):
            head = turn * together + part
            grad_raw, grad_value, grad_rate = late_part(
                load(raw_ref, head), rate_of(head), solver[head], scalings[head, 0:1], solved_v[head],
                errors[head], grad_weighted[head], grad_key[head], state[head], adjoint[head], house,
            )
            out_key[:, :, columns(head)] = grad_raw.reshape(house, tokens, HEAD_DIM).astype(BF16)
            out_value[:, :, columns(head)] = grad_value.reshape(house, tokens, HEAD_DIM).astype(BF16)
            for j in range(house):
                total = jnp.where(
                    lanes == head * house + j, grad_rate[j * tokens : (j + 1) * tokens], total
                )
        return total

    total = lax.fori_loop(0, turns, late_turn, jnp.zeros((tokens, tokens), F32))
    out_rate[...] = jnp.transpose(total)[: house * heads]

    def given(head, carry):
        @pl.when(me != head * spacing)
        def _():
            for args in (decay_args, offset_args, grad_args):
                to_owner(*args, head, me).wait_send()

        return carry

    lax.fori_loop(0, heads, given, 0)

    def handed(user, carry):
        @pl.when(owns & (me != user))
        def _():
            for args in (state_args, adjoint_args):
                to_user(*args, user, mine).wait_send()

        return carry

    lax.fori_loop(0, ctx_count, handed, 0)
    for owner in range(head_count):
        @pl.when((owner <= column) & (column < head_count - 1))
        def _():
            passing(owner, True).wait_send()

        @pl.when((owner >= column) & (column > 0))
        def _():
            passing(owner, False).wait_send()


def hand_over(*refs):
    for source, target in zip(refs[:4], refs[4:]):
        target[...] = source[...]


def shards(queries, key_input, value_input, beta_rates, out_grad, out_weight):
    house, tokens, width = key_input.shape
    heads = width // HEAD_DIM
    rows = house * tokens
    square = (HEAD_DIM, HEAD_DIM)
    ctx_count, head_count = lax.axis_size("ctx"), lax.axis_size("head")
    vmem = pl.BlockSpec(memory_space=pltpu.VMEM)

    def held(*shape, dtype=F32):
        return pltpu.VMEM((heads,) + shape, dtype)

    results = pl.pallas_call(
        functools.partial(kernel, ctx_count, head_count),
        out_shape=(
            jax.ShapeDtypeStruct(queries.shape, BF16),
            jax.ShapeDtypeStruct(key_input.shape, BF16),
            jax.ShapeDtypeStruct(value_input.shape, BF16),
            jax.ShapeDtypeStruct((heads * house, tokens), F32),
        ),
        in_specs=[vmem] * 5 + [pl.BlockSpec(memory_space=pl.ANY)],
        out_specs=(vmem,) * 4,
        scratch_shapes=[
            pltpu.VMEM(out_weight.shape, BF16),
            pltpu.VMEM((tokens, out_grad.shape[1]), BF16),
            pltpu.VMEM((tokens, tokens), F32),
            held(tokens, HEAD_DIM, dtype=BF16),
            held(rows, rows, dtype=BF16),
            held(rows, rows, dtype=SOLVER),
            held(rows, HEAD_DIM),
            held(rows, HEAD_DIM),
            held(*square, dtype=BF16),
            held(*square),
            held(tokens, rows, dtype=BF16),
            held(tokens, HEAD_DIM, dtype=BF16),
            held(*square, dtype=BF16),
            held(8, rows),
            held(rows, HEAD_DIM),
            held(rows, HEAD_DIM),
            held(rows, HEAD_DIM),
            held(*square, dtype=BF16),
            held(*square, dtype=BF16),
            pltpu.VMEM((ctx_count,) + square, BF16),
            pltpu.VMEM((ctx_count,) + square, F32),
            pltpu.VMEM((ctx_count,) + square, BF16),
            pltpu.VMEM((ctx_count,) + square, BF16),
            pltpu.VMEM((ctx_count,) + square, BF16),
            pltpu.SemaphoreType.DMA,
        ]
        + [
            pltpu.SemaphoreType.DMA((count,))
            for count in (head_count,) * 3 + (heads, ctx_count) * 3 + (ctx_count, heads) * 2
        ],
        compiler_params=pltpu.CompilerParams(
            collective_id=0, has_side_effects=True, vmem_limit_bytes=56 * 1024 * 1024
        ),
    )(
        queries,
        key_input,
        value_input,
        beta_rates.reshape(heads * house, tokens),
        out_grad,
        out_weight,
    )
    results = pl.pallas_call(
        hand_over,
        out_shape=[jax.ShapeDtypeStruct(result.shape, result.dtype) for result in results],
        in_specs=[vmem] * 4,
        out_specs=[vmem] * 4,
    )(*results)
    return tuple(results[:3]) + (results[3].reshape(beta_rates.shape),)


def solution(mesh):
    placed = (
        P("ctx", "head"),
        P(None, "ctx", "head"),
        P(None, "ctx", "head"),
        P("head", None, "ctx"),
        P(("ctx", "head"), None),
        P("head", None),
    )
    return jax.shard_map(
        shards,
        mesh=mesh,
        in_specs=placed,
        out_specs=placed[:4],
        check_vma=False,
    )
```

```python
import functools

import jax
import jax.numpy as jnp
from jax import lax
from jax.experimental import pallas as pl
from jax.experimental.pallas import tpu as pltpu
from jax.sharding import PartitionSpec as P

HEAD_DIM = 128
MESH = pl.DeviceIdType.MESH
F32 = jnp.float32
BF16 = jnp.bfloat16
SOLVER = BF16
SPLIT = {
    "inv": "lr", "sk": "l", "sv": "l", "maps": "r", "rd": "lr", "w": "", "gs": "", "q1": "",
    "q2": "", "k1": "", "gw2": "", "un": "r", "gg": "", "k2": "", "k4": "l",
}


def product(left, right, over_left, over_right, split=""):
    def one(a, b):
        return lax.dot_general(
            a, b, (((over_left,), (over_right,)), ((), ())), preferred_element_type=F32
        )

    left_high, right_high = left.astype(BF16), right.astype(BF16)
    total = one(left_high, right_high)
    if "l" in split and left.dtype == F32:
        total += one((left - left_high.astype(F32)).astype(BF16), right_high)
    if "r" in split and right.dtype == F32:
        total += one(left_high, (right - right_high.astype(F32)).astype(BF16))
    return total


def order(shape, axis, tokens, house):
    index = lax.broadcasted_iota(jnp.int32, shape, axis)
    return house * (index % tokens) + index // tokens


def inverse(strict_system, tokens, house):
    shape = strict_system.shape
    rows = shape[0]
    apart = order(shape, 0, tokens, house) ^ order(shape, 1, tokens, house)
    result = -jnp.where(apart == 1, strict_system, 0.0)
    size = 2
    while size < rows:
        corner = jnp.where((apart >= size) & (apart < 2 * size), strict_system, 0.0)
        span = size // house
        split = SPLIT["inv"] if 4 * size >= rows else ""
        if span % 8:
            half = corner + product(corner, result, 1, 0, split)
            result = result - half - product(result, half, 1, 0, split)
        else:
            pairs = (house, tokens // (2 * span), 2, span, rows)

            def second(array):
                return array.reshape(pairs)[:, :, 1].reshape(rows // 2, rows)

            def joined(first, last):
                parts = [part.reshape(pairs[:2] + (1, span, rows)) for part in (first, last)]
                return jnp.concatenate(parts, axis=2).reshape(shape)

            half = second(corner)
            half = half + product(half, result, 1, 0, split)
            lower = second(result)
            whole = joined(jnp.zeros_like(half), half)
            lower = lower - half - product(lower, whole, 1, 0, split)
            result = joined(result.reshape(pairs)[:, :, 0].reshape(rows // 2, rows), lower)
        size *= 2
    return result


def scaling_of(raw):
    raw = raw.astype(F32)
    return lax.rsqrt(jnp.sum(raw * raw, axis=-1, keepdims=True) + 1e-06)


def read_mask(tokens, rows):
    reader = lax.broadcasted_iota(jnp.int32, (tokens, rows), 0)
    return lax.broadcasted_iota(jnp.int32, (tokens, rows), 1) % tokens <= reader


def strict_mask(tokens, house):
    shape = (house * tokens, house * tokens)
    return order(shape, 1, tokens, house) < order(shape, 0, tokens, house)


def solve_part(query, raw, value, rate, rate_row, house):
    tokens = query.shape[0]
    rows = raw.shape[0]
    scaling = scaling_of(raw)
    index = [lax.broadcasted_iota(jnp.int32, (rows, rows), axis) for axis in (0, 1)]
    scaling_row = jnp.sum(jnp.where(index[0] == index[1], scaling, 0.0), axis=0, keepdims=True)
    gram = product(raw, raw, 1, 1)
    gram = jnp.where(strict_mask(tokens, house), gram * scaling * scaling_row, 0.0)
    solver = inverse(gram * rate, tokens, house)
    scaled_raw = raw.astype(F32) * (scaling * rate)
    solved_k = scaled_raw + product(solver * (rate_row * scaling_row), raw, 1, 0, SPLIT["sk"])
    solved_v = value.astype(F32) * rate + product(solver * rate_row, value, 1, 0, SPLIT["sv"])
    both = jnp.concatenate([solved_k * scaling, solved_v * scaling], axis=1)
    maps = product(raw, both, 0, 0, SPLIT["maps"])
    scores = product(query, raw, 1, 1) * (scaling_row * HEAD_DIM ** (-0.5))
    scores = jnp.where(read_mask(tokens, rows), scores, 0.0)
    reading = query.astype(F32) * HEAD_DIM ** (-0.5) - product(scores, solved_k, 1, 0, SPLIT["rd"])
    return (
        gram, solver, solved_k, solved_v, maps[:, :HEAD_DIM], maps[:, HEAD_DIM:], scores, reading,
        jnp.broadcast_to(scaling_row, (8, rows)),
    )


def early_part(query, raw, value, gram, solved_k, solved_v, scores, scaling_row, grad, state):
    tokens = query.shape[0]
    weighted = product(solved_k, state, 1, 0, SPLIT["w"]) - solved_v
    errors = product(raw, state, 1, 0) * scaling_of(raw) - value.astype(F32)
    errors = errors - product(gram, weighted, 1, 0)
    grad_weighted = -product(scores, grad, 0, 0)
    grad_scores = -product(grad, weighted, 1, 1, SPLIT["gs"]) * HEAD_DIM ** (-0.5)
    grad_scores = jnp.where(read_mask(tokens, raw.shape[0]), grad_scores, 0.0)
    grad_query = product(grad, state, 1, 1, SPLIT["q1"]) * HEAD_DIM ** (-0.5)
    grad_query = grad_query + product(grad_scores * scaling_row, raw, 1, 0, SPLIT["q2"])
    grad_key = product(grad_scores, query, 0, 0, SPLIT["k1"])
    return weighted, errors, grad_weighted, grad_query, grad_key


def late_part(
    raw, rate, solver, scaling_row, weighted, errors, grad_weighted, grad_key, state, adjoint, house
):
    tokens = raw.shape[0] // house
    scaling = scaling_of(raw)
    key = raw.astype(F32) * scaling
    grad_weighted = grad_weighted - product(raw, adjoint, 1, 0, SPLIT["gw2"]) * scaling
    unscaled = grad_weighted + product(solver, grad_weighted, 0, 0, SPLIT["un"])
    pulled = unscaled * rate
    grad_rate = jnp.sum(errors * unscaled, axis=1, keepdims=True)
    grad_gram = jnp.where(strict_mask(tokens, house), product(pulled, weighted, 1, 1, SPLIT["gg"]), 0.0)
    grad_gram = (grad_gram + jnp.transpose(grad_gram)) * scaling_row
    rows_side = jnp.concatenate([-weighted, pulled], axis=1)
    state_side = jnp.concatenate([adjoint, state], axis=1)
    grad_key = grad_key + product(rows_side, state_side, 1, 1, SPLIT["k2"])
    grad_key = grad_key - product(grad_gram, raw, 1, 0, SPLIT["k4"])
    along = jnp.sum(grad_key * key, axis=1, keepdims=True)
    grad_raw = scaling * (grad_key - key * along)
    return grad_raw, -pulled, grad_rate


def kernel(
    ctx_count,
    head_count,
    query_ref, raw_ref, value_ref, rate_ref, grad_ref, weight_ref,
    out_query, out_key, out_value, out_rate,
    weight, gathered, rates, grads,
    gram, solver, solved_k, solved_v, decay, offset, scores, reading, local_grad,
    scalings, errors, grad_weighted, grad_key, state, adjoint,
    decay_in, offset_in, grad_in, states, adjoints,
    weight_sem, up_send, down_send, gather_recv,
    decay_send, decay_recv, offset_send, offset_recv, grad_send, grad_recv,
    state_send, state_recv, adjoint_send, adjoint_recv,
):
    me, column = lax.axis_index("ctx"), lax.axis_index("head")
    house, tokens = raw_ref.shape[0], raw_ref.shape[1]
    heads = state.shape[0]
    shard = grad_ref.shape[0]
    rows = house * tokens
    spacing = ctx_count // heads
    owns = lax.rem(me, spacing) == 0
    mine = me // spacing

    weight_copy = pltpu.make_async_copy(weight_ref, weight, weight_sem)
    weight_copy.start()

    barrier = pltpu.get_barrier_semaphore()

    def greet(there, device):
        @pl.when(there)
        def _():
            pl.semaphore_signal(barrier, inc=1, device_id=device, device_id_type=MESH)

        return there.astype(jnp.int32)

    peers = greet(column > 0, {"head": column - 1})
    peers += greet(column < head_count - 1, {"head": column + 1})
    for other in range(ctx_count):
        meets = (me != other) if other % spacing == 0 else (me != other) & owns
        peers += greet(meets, {"ctx": other})
    pl.semaphore_wait(barrier, peers)

    def slot(owner):
        return gathered.at[pl.ds(pl.multiple_of(owner * shard, shard), shard)]

    def passing(owner, up):
        return pltpu.make_async_remote_copy(
            src_ref=slot(owner),
            dst_ref=slot(owner),
            send_sem=(up_send if up else down_send).at[owner],
            recv_sem=gather_recv.at[owner],
            device_id={"head": lax.rem(column + (1 if up else head_count - 1), head_count)},
            device_id_type=MESH,
        )

    gathered[pl.ds(pl.multiple_of(column * shard, shard), shard)] = grad_ref[...]

    def send_on(owner, up):
        @pl.when(column < head_count - 1 if up else column > 0)
        def _():
            passing(owner, up).start()

    send_on(column, True)
    send_on(column, False)

    rates[...] = jnp.zeros_like(rates)
    rates[pl.ds(0, house * heads)] = rate_ref[...]
    rates[...] = jnp.transpose(rates[...])

    lanes = lax.broadcasted_iota(jnp.int32, (tokens, tokens), 1)

    def rate_of(head):
        parts = [
            jnp.sum(jnp.where(lanes == head * house + j, rates[...], 0.0), axis=1, keepdims=True)
            for j in range(house)
        ]
        return jnp.concatenate(parts, axis=0)

    def columns(head):
        return pl.ds(pl.multiple_of(head * HEAD_DIM, HEAD_DIM), HEAD_DIM)

    def load(ref, head):
        return ref[:, :, columns(head)].reshape(rows, HEAD_DIM)

    def to_owner(kept, landing, send, recv, head, source):
        return pltpu.make_async_remote_copy(
            src_ref=kept.at[head], dst_ref=landing.at[source], send_sem=send.at[head],
            recv_sem=recv.at[source], device_id={"ctx": head * spacing}, device_id_type=MESH,
        )

    def give(kept, landing, send, recv, head):
        away = me != head * spacing

        @pl.when(away)
        def _():
            to_owner(kept, landing, send, recv, head, me).start()

        @pl.when(jnp.logical_not(away))
        def _():
            landing[me] = kept[head]

    decay_args = (decay, decay_in, decay_send, decay_recv)
    offset_args = (offset, offset_in, offset_send, offset_recv)
    grad_args = (local_grad, grad_in, grad_send, grad_recv)

    def to_user(made, landing, send, recv, user, head):
        return pltpu.make_async_remote_copy(
            src_ref=made.at[user], dst_ref=landing.at[head], send_sem=send.at[user],
            recv_sem=recv.at[head], device_id={"ctx": user}, device_id_type=MESH,
        )

    def hand_out(made, landing, send, recv, user):
        @pl.when(me != user)
        def _():
            to_user(made, landing, send, recv, user, mine).start()

        @pl.when(me == user)
        def _():
            landing[mine] = made[user]

    state_args = (states, state, state_send, state_recv)
    adjoint_args = (adjoints, adjoint, adjoint_send, adjoint_recv)

    def solve_head(head):
        results = solve_part(
            query_ref[:, columns(head)], load(raw_ref, head), load(value_ref, head), rate_of(head),
            jnp.concatenate([rate_ref[pl.ds(head * house + j, 1)] for j in range(house)], axis=1), house,
        )
        kept = (gram, solver, solved_k, solved_v, decay, offset, scores, reading, scalings)
        for ref, result in zip(kept, results):
            ref[head] = result.astype(ref.dtype)

    together = 2 if heads % 2 == 0 else 1
    turns = heads // together

    def gather_turn(turn):
        for owner, up in ((column - turn, True), (column + turn, False)):
            @pl.when((owner >= 0) & (owner < head_count))
            def _():
                passing(owner, up).wait_recv()
                send_on(owner, up)

    def solve_turn(turn, carry):
        for part in range(together):
            solve_head(turn * together + part)
        for part in range(together):
            give(*decay_args, turn * together + part)
            give(*offset_args, turn * together + part)

        @pl.when((turn + 1) < head_count)
        def _():
            gather_turn(turn + 1)

        return carry

    lax.fori_loop(0, turns, solve_turn, 0)
    for turn in range(turns + 1, head_count):
        gather_turn(turn)

    weight_copy.wait()

    def grad_turn(turn, carry):
        part = pl.ds(pl.multiple_of(turn * together * HEAD_DIM, HEAD_DIM), together * HEAD_DIM)
        block = product(gathered[...], weight[part, :], 1, 1).astype(BF16)
        for index in range(together):
            head = turn * together + index
            grad = block[:, index * HEAD_DIM : (index + 1) * HEAD_DIM]
            grads[head] = grad
            local_grad[head] = product(reading[head], grad, 0, 0).astype(BF16)
            give(*grad_args, head)
        return carry

    lax.fori_loop(0, turns, grad_turn, 0)

    @pl.when(owns)
    def _():
        def arrive(args, source):
            @pl.when(me != source)
            def _():
                to_owner(*args, mine, source).wait_recv()

        def forward(user, held):
            states[user] = held.astype(BF16)
            hand_out(*state_args, user)
            arrive(decay_args, user)
            arrive(offset_args, user)
            return held + offset_in[user] - product(decay_in[user], held, 1, 0)

        zero = jnp.zeros((HEAD_DIM, HEAD_DIM), F32)
        lax.fori_loop(0, ctx_count, forward, zero)

        def backward(step, held):
            user = ctx_count - 1 - step
            adjoints[user] = held.astype(BF16)
            hand_out(*adjoint_args, user)
            arrive(grad_args, user)
            return held + grad_in[user] - product(decay_in[user], held, 0, 0)

        lax.fori_loop(0, ctx_count, backward, zero)

    def early_head(head):
        @pl.when(me != head * spacing)
        def _():
            to_user(*state_args, me, head).wait_recv()

    def early_turn(turn, carry):
        for part in range(together):
            early_head(turn * together + part)
        for part in range(together):
            head = turn * together + part
            results = early_part(
                query_ref[:, columns(head)], load(raw_ref, head), load(value_ref, head), gram[head],
                solved_k[head], solved_v[head], scores[head], scalings[head, 0:1], grads[head], state[head],
            )
            solved_v[head], errors[head], grad_weighted[head] = results[:3]
            out_query[:, columns(head)] = results[3].astype(BF16)
            grad_key[head] = results[4]
        return carry

    lax.fori_loop(0, turns, early_turn, 0)

    def late_turn(turn, total):
        for part in range(together):
            head = turn * together + part

            @pl.when(me != head * spacing)
            def _():
                to_user(*adjoint_args, me, head).wait_recv()

        for part in range(together):
            head = turn * together + part
            grad_raw, grad_value, grad_rate = late_part(
                load(raw_ref, head), rate_of(head), solver[head], scalings[head, 0:1], solved_v[head],
                errors[head], grad_weighted[head], grad_key[head], state[head], adjoint[head], house,
            )
            out_key[:, :, columns(head)] = grad_raw.reshape(house, tokens, HEAD_DIM).astype(BF16)
            out_value[:, :, columns(head)] = grad_value.reshape(house, tokens, HEAD_DIM).astype(BF16)
            for j in range(house):
                total = jnp.where(
                    lanes == head * house + j, grad_rate[j * tokens : (j + 1) * tokens], total
                )
        return total

    total = lax.fori_loop(0, turns, late_turn, jnp.zeros((tokens, tokens), F32))
    out_rate[...] = jnp.transpose(total)[: house * heads]

    def given(head, carry):
        @pl.when(me != head * spacing)
        def _():
            for args in (decay_args, offset_args, grad_args):
                to_owner(*args, head, me).wait_send()

        return carry

    lax.fori_loop(0, heads, given, 0)

    def handed(user, carry):
        @pl.when(owns & (me != user))
        def _():
            for args in (state_args, adjoint_args):
                to_user(*args, user, mine).wait_send()

        return carry

    lax.fori_loop(0, ctx_count, handed, 0)
    for owner in range(head_count):
        @pl.when((owner <= column) & (column < head_count - 1))
        def _():
            passing(owner, True).wait_send()

        @pl.when((owner >= column) & (column > 0))
        def _():
            passing(owner, False).wait_send()


def hand_over(*refs):
    for source, target in zip(refs[:4], refs[4:]):
        target[...] = source[...]


def shards(queries, key_input, value_input, beta_rates, out_grad, out_weight):
    house, tokens, width = key_input.shape
    heads = width // HEAD_DIM
    rows = house * tokens
    square = (HEAD_DIM, HEAD_DIM)
    ctx_count, head_count = lax.axis_size("ctx"), lax.axis_size("head")
    vmem = pl.BlockSpec(memory_space=pltpu.VMEM)

    def held(*shape, dtype=F32):
        return pltpu.VMEM((heads,) + shape, dtype)

    results = pl.pallas_call(
        functools.partial(kernel, ctx_count, head_count),
        out_shape=(
            jax.ShapeDtypeStruct(queries.shape, BF16),
            jax.ShapeDtypeStruct(key_input.shape, BF16),
            jax.ShapeDtypeStruct(value_input.shape, BF16),
            jax.ShapeDtypeStruct((heads * house, tokens), F32),
        ),
        in_specs=[vmem] * 5 + [pl.BlockSpec(memory_space=pl.ANY)],
        out_specs=(vmem,) * 4,
        scratch_shapes=[
            pltpu.VMEM(out_weight.shape, BF16),
            pltpu.VMEM((tokens, out_grad.shape[1]), BF16),
            pltpu.VMEM((tokens, tokens), F32),
            held(tokens, HEAD_DIM, dtype=BF16),
            held(rows, rows, dtype=BF16),
            held(rows, rows, dtype=SOLVER),
            held(rows, HEAD_DIM),
            held(rows, HEAD_DIM),
            held(*square, dtype=BF16),
            held(*square, dtype=BF16),
            held(tokens, rows, dtype=BF16),
            held(tokens, HEAD_DIM, dtype=BF16),
            held(*square, dtype=BF16),
            held(8, rows),
            held(rows, HEAD_DIM),
            held(rows, HEAD_DIM),
            held(rows, HEAD_DIM),
            held(*square, dtype=BF16),
            held(*square, dtype=BF16),
            pltpu.VMEM((ctx_count,) + square, BF16),
            pltpu.VMEM((ctx_count,) + square, BF16),
            pltpu.VMEM((ctx_count,) + square, BF16),
            pltpu.VMEM((ctx_count,) + square, BF16),
            pltpu.VMEM((ctx_count,) + square, BF16),
            pltpu.SemaphoreType.DMA,
        ]
        + [
            pltpu.SemaphoreType.DMA((count,))
            for count in (head_count,) * 3 + (heads, ctx_count) * 3 + (ctx_count, heads) * 2
        ],
        compiler_params=pltpu.CompilerParams(
            collective_id=0, has_side_effects=True, vmem_limit_bytes=56 * 1024 * 1024
        ),
    )(
        queries,
        key_input,
        value_input,
        beta_rates.reshape(heads * house, tokens),
        out_grad,
        out_weight,
    )
    results = pl.pallas_call(
        hand_over,
        out_shape=[jax.ShapeDtypeStruct(result.shape, result.dtype) for result in results],
        in_specs=[vmem] * 4,
        out_specs=[vmem] * 4,
    )(*results)
    return tuple(results[:3]) + (results[3].reshape(beta_rates.shape),)


def solution(mesh):
    placed = (
        P("ctx", "head"),
        P(None, "ctx", "head"),
        P(None, "ctx", "head"),
        P("head", None, "ctx"),
        P(("ctx", "head"), None),
        P("head", None),
    )
    return jax.shard_map(
        shards,
        mesh=mesh,
        in_specs=placed,
        out_specs=placed[:4],
        check_vma=False,
    )
```
